128 devices in a mesh: hi: 16 (over z, x), lo: 8 (over y, core).
Axes of the slice: x: 4, y: 4, z: 4, core: 2. Of those that a mesh axis runs over, the one named last changes fastest.
Arguments:
- panel: float32 [2097152, 128], P(('hi', 'lo')), may hold values from -6 to 6
- signs: int32 [2097152], P(('hi', 'lo')), may hold values from -1 to 1, as said below
- sample_rows: int32 [8192], replicated, may hold values from 0 to 2097151, as said below
Outputs:
- q_factor: float32 [8192, 128], P(('hi', 'lo'))
- r_factor: float32 [128, 128], replicated
The draws below stay inside these ranges and needn't reach their ends.
Inputs may be any that keep to these rules, and one draw needn't show every extreme that they name: `sample_rows`: entries 64 * d to 64 * (d + 1) - 1 are rows in d * 16384 to (d + 1) * 16384 - 1, drawn evenly with replacement; the value 0 and the value 2097152 - 1 occur in every draw. `signs`: every entry is -1 or 1.
All inputs are finite; a program needn't handle non-finite values.
Results may differ from the reference program's by a relative error of at most 0.000076.
Values sent between devices are 32-bit elements; how exact they have to be, the bound alone decides.
A program may use at most 128 MiB of HBM per device.

```python
import math
import jax
import jax.numpy as jnp
from jax import lax

COLS = 128
ROWS_DEV = 16384
LOCAL_A = 128
K_DEV = 64
M = 2097152
K = 8192
N_HI = 16
N_LO = 8


def draw_signs(key, part):
    key = jax.random.fold_in(key, 11)
    return (2 * jax.random.randint(key, (M,), 0, 2) - 1).astype(jnp.int32)


def draw_sample_rows(key, part):
    key = jax.random.fold_in(key, 23)
    blocks = M // ROWS_DEV
    within = jax.random.randint(key, (blocks, K_DEV), 0, ROWS_DEV)
    within = within.at[0, 0].set(0)
    within = within.at[blocks - 1, K_DEV - 1].set(ROWS_DEV - 1)
    starts = jnp.arange(blocks, dtype=jnp.int32)[:, None] * ROWS_DEV
    return (starts + within).reshape(K_DEV * blocks).astype(jnp.int32)


def shard_levels(key, extent, split, least, top_value):
    gain = 1.0
    for axis_at, shards_of in split:
        heights = jax.random.uniform(jax.random.fold_in(jax.random.fold_in(key, 6), axis_at), (shards_of,), jnp.float32, least / len(split), top_value / len(split))
        gain = gain * jnp.repeat(jnp.exp(heights), extent[axis_at] // shards_of).reshape((-1,) + (1,) * (len(extent) - 1 - axis_at))
    return gain


def bell_draw(rng, shape, spread, reach, cuts=(), held_as=jnp.bfloat16):
    array = spread * jax.random.normal(rng, shape, jnp.float32)
    if cuts:
        array = array * shard_levels(rng, shape, cuts, -0.22, 0.18)
    return jnp.clip(array, -reach, reach).astype(held_as)


def setup_inputs(seed: int = 0) -> dict:
    seeds = jax.random.split(jax.random.key(seed), 4)
    return {
        "panel": bell_draw(seeds[0], (M, COLS), 1.0, 6.0, ((0, 128),), jnp.float32),
        "signs": draw_signs(jax.random.fold_in(seeds[3], 71), 0),
        "sample_rows": draw_sample_rows(jax.random.fold_in(seeds[3], 71), 0),
    }


def hadamard(order):
    index = jnp.arange(order, dtype=jnp.int32)
    common = jnp.bitwise_and(index[:, None], index[None, :])
    parity = jnp.zeros((order, order), jnp.int32)
    for bit_place in range(max(order.bit_length() - 1, 1)):
        parity = parity + jnp.bitwise_and(jnp.right_shift(common, bit_place), 1)
    return jnp.where(parity % 2 == 0, 1.0, -1.0).astype(jnp.float32)

def reference(panel, signs, sample_rows):
    highest = lax.Precision.HIGHEST
    device_count = N_HI * N_LO
    inner = ROWS_DEV // LOCAL_A
    signed = panel * signs[:, None].astype(jnp.float32)
    blocks = signed.reshape(device_count, LOCAL_A, inner, COLS)
    blocks = jnp.einsum('ij,jabc->iabc', hadamard(device_count), blocks, precision=highest)
    blocks = jnp.einsum('ij,ajbc->aibc', hadamard(LOCAL_A), blocks, precision=highest)
    blocks = jnp.einsum('ij,abjc->abic', hadamard(inner), blocks, precision=highest)
    transformed = blocks.reshape(M, COLS) / math.sqrt(M)
    sketch = jnp.take(transformed, sample_rows, axis=0)
    gram = jnp.dot(sketch.T.astype(jnp.float32), sketch.astype(jnp.float32), precision=highest, preferred_element_type=jnp.float32) / K
    lower = jnp.linalg.cholesky(gram)
    q_factor = lax.linalg.triangular_solve(lower, sketch, left_side=False, lower=True, transpose_a=True)
    return (q_factor, lower.T)
```

```python
import functools
import math

import jax
import jax.numpy as jnp
from jax import lax
from jax.experimental import pallas as pl
from jax.experimental.pallas import tpu as pltpu
from jax.sharding import PartitionSpec as P

MESH = pl.DeviceIdType.MESH
COLS = 128
MIX = 256
LOADS = 8
BLOCK = 16
PARTS = ((0, 24), (24, 24), (48, 16))
ORDERS = ((0, 1, 2), (1, 2, 0), (2, 0, 1))
GRAM_PARTS = ((0, 48), (48, 40), (88, 40))


def parity_sign(value, bits):
    total = value & 1
    for place in range(1, bits):
        total = total + ((value >> place) & 1)
    return 1.0 - 2.0 * (total & 1).astype(jnp.float32)


def hadamard(order):
    shape = (order, order)
    common = lax.broadcasted_iota(jnp.int32, shape, 0) & lax.broadcasted_iota(jnp.int32, shape, 1)
    return parity_sign(common, order.bit_length() - 1)


def butterfly(values):
    half = 1
    values = list(values)
    while half < len(values):
        for at in range(len(values)):
            if at & half == 0:
                low, high = values[at], values[at + half]
                values[at], values[at + half] = low + high, low - high
        half *= 2
    return values


def split_three(value):
    first = value.astype(jnp.bfloat16).astype(jnp.float32)
    rest = value - first
    second = rest.astype(jnp.bfloat16).astype(jnp.float32)
    return first, second, rest - second


def widen(value, width):
    return jnp.concatenate([value] * (width // COLS), axis=1)


def eliminate(rest, put):
    order, width = rest.shape
    row_at = lax.broadcasted_iota(jnp.int32, (BLOCK, COLS), 0)
    for step in range(order // BLOCK):
        base = step * BLOCK
        rows = rest[:BLOCK]
        columns = [
            jnp.broadcast_to(rows[:, base + m : base + m + 1], (BLOCK, COLS)) for m in range(BLOCK)
        ]
        pivots = jnp.ones((BLOCK, COLS), jnp.float32)
        for j in range(BLOCK):
            pivot = jnp.broadcast_to(columns[j][j : j + 1, :], (BLOCK, COLS))
            pivots = jnp.where(row_at == j, pivot, pivots)
            if j < BLOCK - 1:
                factor = jnp.where(row_at > j, columns[j] * (1.0 / pivot), 0.0)
                for m in range(j + 1, BLOCK):
                    columns[m] = columns[m] - factor * jnp.broadcast_to(
                        columns[m][j : j + 1, :], (BLOCK, COLS)
                    )
                rows = rows - widen(factor, width) * jnp.broadcast_to(
                    rows[j : j + 1, :], (BLOCK, width)
                )
        done = rows * widen(lax.rsqrt(pivots), width)
        put(base, done)
        if base + BLOCK < order:
            a, b, c = split_three(done)
            left = jnp.concatenate([t[:, :COLS] for t in (a, a, a, b, b, c)], axis=0)
            right = jnp.concatenate([a, b, c, a, b, a], axis=0).astype(jnp.bfloat16)
            turned = jnp.transpose(left)[base + BLOCK :, :].astype(jnp.bfloat16)
            rest = rest[BLOCK:] - jnp.dot(turned, right, preferred_element_type=jnp.float32)


def kernel(
    scale, samples, panel_hbm, sign_ref, index_hbm, q_ref, r_ref,
    panel, work, mix, index, away, near, home, land1, sum1, land2, sum2, land3, sketch,
    gram, gram_land, core_land, augmented,
    load_sem, index_sem, core_send, core_recv, s1, r1, s2, r2, s3, r3, gs, gr, gcs, gcr,
):
    hi, lo = lax.axis_index("hi"), lax.axis_index("lo")
    core = lo % 2
    place = (hi // 4, hi % 4, lo // 2)

    def device(coords, which):
        return (coords[0] * 4 + coords[1], coords[2] * 2 + which)

    def peer(axis, delta):
        coords = list(place)
        coords[axis] = coords[axis] ^ delta
        return device(coords, core)

    other = device(place, 1 - core)

    barrier = pltpu.get_barrier_semaphore()
    pl.semaphore_signal(barrier, inc=1, device_id=other, device_id_type=MESH)
    for axis in range(3):
        for delta in range(1, 4):
            pl.semaphore_signal(barrier, inc=1, device_id=peer(axis, delta), device_id_type=MESH)

    rows = panel.shape[0]
    outer = rows // MIX
    per_load = outer // LOADS
    piece = rows // LOADS

    def load(at):
        span = pl.ds(pl.multiple_of(at * piece, piece), piece)
        return pltpu.make_async_copy(panel_hbm.at[span], panel.at[span], load_sem.at[at])

    for at in range(LOADS):
        load(at).start()
    index_copy = pltpu.make_async_copy(index_hbm, index, index_sem)
    index_copy.start()
    mix[...] = hadamard(MIX).astype(jnp.bfloat16)

    def mix_group(at, carry):
        load(at).wait()
        for inner in range(per_load):
            start = pl.multiple_of((at * per_load + inner) * MIX, MIX)
            value = panel[pl.ds(start, MIX), :]
            high = value.astype(jnp.bfloat16)
            low = (value - high.astype(jnp.float32)).astype(jnp.bfloat16)
            signs = sign_ref[pl.ds(at * per_load + inner, 1), :].astype(jnp.float32)
            signed_mix = mix[...] * jnp.broadcast_to(signs, (MIX, MIX)).astype(jnp.bfloat16)
            mixed = jnp.dot(
                signed_mix, jnp.concatenate([high, low], axis=1), preferred_element_type=jnp.float32
            )
            work[pl.ds(start, MIX), :] = mixed[:, :COLS] + mixed[:, COLS:]
        return carry

    lax.fori_loop(0, LOADS, mix_group, 0)

    def butterflies(outer_stride, stride):
        def group(at, carry):
            def tile(t, carry):
                base = pl.multiple_of(at * outer_stride + t * 8, 8)
                spans = [pl.ds(pl.multiple_of(base + m * stride, 8), 8) for m in range(8)]
                for span, value in zip(spans, butterfly([work[span, :] for span in spans])):
                    work[span, :] = value
                return carry

            return lax.fori_loop(0, MIX // 8, tile, carry, unroll=4)

        lax.fori_loop(0, 8, group, 0)

    butterflies(8 * MIX, MIX)
    butterflies(MIX, 8 * MIX)
    index_copy.wait()

    def gather(target, part, delta, which):
        offset, count = PARTS[part]
        a, b, c = ORDERS[part]

        def one(j, carry):
            coords = [None] * 3
            coords[a] = place[a] ^ delta
            coords[b] = place[b] ^ (j // 4)
            coords[c] = place[c] ^ (j % 4)
            chip = coords[0] * 16 + coords[1] * 4 + coords[2]
            base = (chip * 2 + which) * samples + offset
            to = pl.multiple_of(j * count, 8)
            for k in range(count):
                row = index[base + k] & (rows - 1)
                target[part][pl.ds(delta * 16 * count + to + k, 1), :] = work[pl.ds(row, 1), :]
            return carry

        lax.fori_loop(0, 16, one, 0)

    def chunk(ref, part, delta):
        size = 16 * PARTS[part][1]
        return ref[part].at[pl.ds(delta * size, size)]

    def send(source, target, send_sem, recv_sem, to):
        return pltpu.make_async_remote_copy(
            src_ref=source, dst_ref=target, send_sem=send_sem, recv_sem=recv_sem,
            device_id=to, device_id_type=MESH,
        )

    pl.semaphore_wait(barrier, 10)
    sequence = [(part, delta) for delta in (1, 2, 3, 0) for part in range(3)]
    core_copies = {}
    for part, delta in sequence:
        gather(away, part, delta, 1 - core)
        at = part * 4 + delta
        copy = send(
            chunk(away, part, delta), chunk(near, part, delta),
            core_send.at[at], core_recv.at[at], other,
        )
        copy.start()
        core_copies[part, delta] = copy

    core_sign = 1.0 - 2.0 * core.astype(jnp.float32)
    copies1 = {}
    for part, delta in sequence:
        gather(home, part, delta, core)
        core_copies[part, delta].wait_recv()
        mine, theirs = chunk(home, part, delta), chunk(near, part, delta)
        mine[...] = theirs[...] + core_sign * mine[...]
        if delta:
            at = part * 3 + delta - 1
            size = 16 * PARTS[part][1]
            copy = send(
                mine, land1[part].at[pl.ds((delta - 1) * size, size)],
                s1.at[at], r1.at[at], peer(ORDERS[part][0], delta),
            )
            copy.start()
            copies1[part, delta] = copy

    def reduced(own, landed, size, axis, start, count):
        here = place[axis]
        total = parity_sign(here, 2) * own[pl.ds(start, count), :]
        for delta in range(1, 4):
            sign = parity_sign(here & (here ^ delta), 2)
            total = total + sign * landed[pl.ds((delta - 1) * size + start, count), :]
        return total

    copies2 = {}
    for part in range(3):
        count = PARTS[part][1]
        for delta in range(1, 4):
            copies1[part, delta].wait_recv()
        for delta in (1, 2, 3, 0):
            span = pl.ds(delta * 4 * count, 4 * count)
            sum1[part][span, :] = reduced(
                home[part], land1[part], 16 * count, ORDERS[part][0], delta * 4 * count, 4 * count
            )
            if delta:
                at = part * 3 + delta - 1
                copy = send(
                    sum1[part].at[span],
                    land2[part].at[pl.ds((delta - 1) * 4 * count, 4 * count)],
                    s2.at[at], r2.at[at], peer(ORDERS[part][1], delta),
                )
                copy.start()
                copies2[part, delta] = copy

    copies3 = {}
    for part in range(3):
        count = PARTS[part][1]
        for delta in range(1, 4):
            copies2[part, delta].wait_recv()
        for delta in (1, 2, 3, 0):
            span = pl.ds(delta * count, count)
            sum2[part][span, :] = reduced(
                sum1[part], land2[part], 4 * count, ORDERS[part][1], delta * count, count
            )
            if delta:
                at = part * 3 + delta - 1
                copy = send(
                    sum2[part].at[span], land3[part].at[pl.ds((delta - 1) * count, count)],
                    s3.at[at], r3.at[at], peer(ORDERS[part][2], delta),
                )
                copy.start()
                copies3[part, delta] = copy

    for part in range(3):
        offset, count = PARTS[part]
        for delta in range(1, 4):
            copies3[part, delta].wait_recv()
        sketch[pl.ds(offset, count), :] = scale * reduced(
            sum2[part], land3[part], count, ORDERS[part][2], 0, count
        )

    rows_here = jnp.concatenate(
        [sketch[...], jnp.zeros((COLS - samples, COLS), jnp.float32)], axis=0
    )
    turned = jnp.transpose(rows_here)
    device_total = lax.axis_size("hi") * lax.axis_size("lo")
    gram[0] = jnp.dot(
        turned, rows_here, precision=lax.Precision.HIGHEST, preferred_element_type=jnp.float32
    ) * (1.0 / (samples * device_total))

    core_gram = send(gram.at[0], core_land, gcs, gcr, other)
    core_gram.start()
    core_gram.wait_recv()
    gram[1] = gram[0] + core_land[...]
    gram_copies = []
    for stage in range(3):
        now = {}
        for part in range(3):
            offset, count = GRAM_PARTS[part]
            span = pl.ds(offset, count)
            for delta in range(1, 4):
                at = stage * 9 + part * 3 + delta - 1
                copy = send(
                    gram.at[stage + 1, span], gram_land.at[stage * 3 + delta - 1, span],
                    gs.at[at], gr.at[at], peer(ORDERS[part][stage], delta),
                )
                copy.start()
                now[part, delta] = copy
                gram_copies.append(copy)
        for part in range(3):
            offset, count = GRAM_PARTS[part]
            span = pl.ds(offset, count)
            for delta in range(1, 4):
                now[part, delta].wait_recv()
            own = gram[stage + 1, span, :]
            one, two, three = (gram_land[stage * 3 + d, span, :] for d in range(3))
            gram[stage + 2, span, :] = (own + two) + (one + three)

    def put(base, value):
        augmented[base : base + BLOCK, :] = value

    eliminate(jnp.concatenate([gram[4], turned], axis=1), put)
    row_at = lax.broadcasted_iota(jnp.int32, (COLS, COLS), 0)
    col_at = lax.broadcasted_iota(jnp.int32, (COLS, COLS), 1)
    r_ref[...] = jnp.where(row_at <= col_at, augmented[:, :COLS], 0.0)
    q_ref[...] = jnp.transpose(augmented[:, COLS:])[:samples, :]

    for group in (core_copies, copies1, copies2, copies3):
        for copy in group.values():
            copy.wait_send()
    core_gram.wait_send()
    for copy in gram_copies:
        copy.wait_send()


def shards(panel, signs, sample_rows):
    rows, cols = panel.shape
    devices = lax.axis_size(("hi", "lo"))
    samples = sample_rows.shape[0] // devices
    counts = [count for _, count in PARTS]
    f32 = jnp.float32

    def buffers(blocks):
        return [pltpu.VMEM((blocks * count, cols), f32) for count in counts]

    dma = pltpu.SemaphoreType.DMA
    vmem = pl.BlockSpec(memory_space=pltpu.VMEM)
    hbm = pl.BlockSpec(memory_space=pl.ANY)
    return pl.pallas_call(
        functools.partial(kernel, 1.0 / math.sqrt(rows * devices), samples),
        out_shape=(
            jax.ShapeDtypeStruct((samples, cols), f32),
            jax.ShapeDtypeStruct((cols, cols), f32),
        ),
        in_specs=[hbm, vmem, hbm],
        out_specs=(vmem, vmem),
        scratch_shapes=[
            pltpu.VMEM((rows, cols), f32),
            pltpu.VMEM((rows, cols), f32),
            pltpu.VMEM((MIX, MIX), jnp.bfloat16),
            pltpu.SMEM(sample_rows.shape, jnp.int32),
            buffers(64), buffers(64), buffers(64),
            buffers(48), buffers(16), buffers(12), buffers(4), buffers(3),
            pltpu.VMEM((samples, cols), f32),
            pltpu.VMEM((5, cols, cols), f32),
            pltpu.VMEM((9, cols, cols), f32),
            pltpu.VMEM((cols, cols), f32),
            pltpu.VMEM((cols, 2 * cols), f32),
            dma((LOADS,)), dma, dma((12,)), dma((12,)),
            dma((9,)), dma((9,)), dma((9,)), dma((9,)), dma((9,)), dma((9,)),
            dma((27,)), dma((27,)), dma, dma,
        ],
        compiler_params=pltpu.CompilerParams(
            collective_id=0, has_side_effects=True, vmem_limit_bytes=48 * 2**20
        ),
        name="sketch_qr",
    )(panel, signs.reshape(rows // MIX, MIX), sample_rows)


def solution(mesh):
    placed = (P(("hi", "lo"), None), P(("hi", "lo")), P())
    return jax.shard_map(
        shards, mesh=mesh, in_specs=placed, out_specs=(P(("hi", "lo"), None), P()), check_vma=False
    )
```

```python
import functools
import math

import jax
import jax.numpy as jnp
from jax import lax
from jax.experimental import pallas as pl
from jax.experimental.pallas import tpu as pltpu
from jax.sharding import PartitionSpec as P

MESH = pl.DeviceIdType.MESH
COLS = 128
MIX = 256
LOADS = 8
BLOCK = 16
PARTS = ((0, 24), (24, 24), (48, 16))
ORDERS = ((0, 1, 2), (1, 2, 0), (2, 0, 1))
GRAM_PARTS = ((0, 48), (48, 40), (88, 40))


def parity_sign(value, bits):
    total = value & 1
    for place in range(1, bits):
        total = total + ((value >> place) & 1)
    return 1.0 - 2.0 * (total & 1).astype(jnp.float32)


def hadamard(order):
    shape = (order, order)
    common = lax.broadcasted_iota(jnp.int32, shape, 0) & lax.broadcasted_iota(jnp.int32, shape, 1)
    return parity_sign(common, order.bit_length() - 1)


def butterfly(values):
    half = 1
    values = list(values)
    while half < len(values):
        for at in range(len(values)):
            if at & half == 0:
                low, high = values[at], values[at + half]
                values[at], values[at + half] = low + high, low - high
        half *= 2
    return values


def split_three(value):
    first = value.astype(jnp.bfloat16).astype(jnp.float32)
    rest = value - first
    second = rest.astype(jnp.bfloat16).astype(jnp.float32)
    return first, second, rest - second


def widen(value, width):
    return jnp.concatenate([value] * (width // COLS), axis=1)


def eliminate(rest, put):
    order, width = rest.shape
    row_at = lax.broadcasted_iota(jnp.int32, (BLOCK, COLS), 0)
    for step in range(order // BLOCK):
        base = step * BLOCK
        rows = rest[:BLOCK]
        columns = [
            jnp.broadcast_to(rows[:, base + m : base + m + 1], (BLOCK, COLS)) for m in range(BLOCK)
        ]
        pivots = jnp.ones((BLOCK, COLS), jnp.float32)
        for j in range(BLOCK):
            pivot = jnp.broadcast_to(columns[j][j : j + 1, :], (BLOCK, COLS))
            pivots = jnp.where(row_at == j, pivot, pivots)
            if j < BLOCK - 1:
                factor = jnp.where(row_at > j, columns[j] * (1.0 / pivot), 0.0)
                for m in range(j + 1, BLOCK):
                    columns[m] = columns[m] - factor * jnp.broadcast_to(
                        columns[m][j : j + 1, :], (BLOCK, COLS)
                    )
                rows = rows - widen(factor, width) * jnp.broadcast_to(
                    rows[j : j + 1, :], (BLOCK, width)
                )
        done = rows * widen(lax.rsqrt(pivots), width)
        put(base, done)
        if base + BLOCK < order:
            a, b, c = split_three(done)
            left = jnp.concatenate([t[:, :COLS] for t in (a, a, a, b, b, c)], axis=0)
            right = jnp.concatenate([a, b, c, a, b, a], axis=0).astype(jnp.bfloat16)
            turned = jnp.transpose(left)[base + BLOCK :, :].astype(jnp.bfloat16)
            rest = rest[BLOCK:] - jnp.dot(turned, right, preferred_element_type=jnp.float32)


def kernel(
    scale, samples, panel_hbm, sign_hbm, index_hbm, q_ref, r_ref,
    panel, work, mix, sign_ref, index, away, near, home, land1, sum1, land2, sum2, land3, sketch,
    gram, gram_land, core_land, augmented,
    load_sem, sign_sem, index_sem, core_send, core_recv, s1, r1, s2, r2, s3, r3, gs, gr, gcs, gcr,
):
    hi, lo = lax.axis_index("hi"), lax.axis_index("lo")
    core = lo % 2
    place = (hi // 4, hi % 4, lo // 2)

    def device(coords, which):
        return (coords[0] * 4 + coords[1], coords[2] * 2 + which)

    def peer(axis, delta):
        coords = list(place)
        coords[axis] = coords[axis] ^ delta
        return device(coords, core)

    other = device(place, 1 - core)

    barrier = pltpu.get_barrier_semaphore()
    pl.semaphore_signal(barrier, inc=1, device_id=other, device_id_type=MESH)
    for axis in range(3):
        for delta in range(1, 4):
            pl.semaphore_signal(barrier, inc=1, device_id=peer(axis, delta), device_id_type=MESH)

    rows = panel.shape[0]
    outer = rows // MIX
    per_load = outer // LOADS
    piece = rows // LOADS

    def load(at):
        span = pl.ds(pl.multiple_of(at * piece, piece), piece)
        return pltpu.make_async_copy(panel_hbm.at[span], panel.at[span], load_sem.at[at])

    sign_copy = pltpu.make_async_copy(sign_hbm, sign_ref, sign_sem)
    sign_copy.start()
    for at in range(LOADS):
        load(at).start()
    index_copy = pltpu.make_async_copy(index_hbm, index, index_sem)
    index_copy.start()
    mix[...] = hadamard(MIX).astype(jnp.bfloat16)
    sign_copy.wait()

    def mix_group(at, carry):
        load(at).wait()
        for inner in range(per_load):
            start = pl.multiple_of((at * per_load + inner) * MIX, MIX)
            value = panel[pl.ds(start, MIX), :]
            high = value.astype(jnp.bfloat16)
            low = (value - high.astype(jnp.float32)).astype(jnp.bfloat16)
            line = (at * per_load + inner) * (MIX // COLS)
            signs = jnp.concatenate(
                [sign_ref[pl.ds(line + m, 1), :] for m in range(MIX // COLS)], axis=1
            ).astype(jnp.float32)
            signed_mix = mix[...] * jnp.broadcast_to(signs, (MIX, MIX)).astype(jnp.bfloat16)
            mixed = jnp.dot(
                signed_mix, jnp.concatenate([high, low], axis=1), preferred_element_type=jnp.float32
            )
            work[pl.ds(start, MIX), :] = mixed[:, :COLS] + mixed[:, COLS:]
        return carry

    lax.fori_loop(0, LOADS, mix_group, 0)

    def butterflies(outer_stride, stride):
        def group(at, carry):
            def tile(t, carry):
                base = pl.multiple_of(at * outer_stride + t * 8, 8)
                spans = [pl.ds(pl.multiple_of(base + m * stride, 8), 8) for m in range(8)]
                for span, value in zip(spans, butterfly([work[span, :] for span in spans])):
                    work[span, :] = value
                return carry

            return lax.fori_loop(0, MIX // 8, tile, carry, unroll=4)

        lax.fori_loop(0, 8, group, 0)

    butterflies(8 * MIX, MIX)
    butterflies(MIX, 8 * MIX)
    index_copy.wait()

    def gather(target, part, delta, which):
        offset, count = PARTS[part]
        a, b, c = ORDERS[part]

        def one(j, carry):
            coords = [None] * 3
            coords[a] = place[a] ^ delta
            coords[b] = place[b] ^ (j // 4)
            coords[c] = place[c] ^ (j % 4)
            chip = coords[0] * 16 + coords[1] * 4 + coords[2]
            base = (chip * 2 + which) * samples + offset
            to = pl.multiple_of(j * count, 8)
            for k in range(count):
                row = index[base + k] & (rows - 1)
                target[part][pl.ds(delta * 16 * count + to + k, 1), :] = work[pl.ds(row, 1), :]
            return carry

        lax.fori_loop(0, 16, one, 0)

    def chunk(ref, part, delta):
        size = 16 * PARTS[part][1]
        return ref[part].at[pl.ds(delta * size, size)]

    def send(source, target, send_sem, recv_sem, to):
        return pltpu.make_async_remote_copy(
            src_ref=source, dst_ref=target, send_sem=send_sem, recv_sem=recv_sem,
            device_id=to, device_id_type=MESH,
        )

    pl.semaphore_wait(barrier, 10)
    sequence = [(part, delta) for delta in (1, 2, 3, 0) for part in range(3)]
    core_sign = 1.0 - 2.0 * core.astype(jnp.float32)
    core_copies, copies1 = {}, {}

    def give(part, delta):
        gather(away, part, delta, 1 - core)
        at = part * 4 + delta
        copy = send(
            chunk(away, part, delta), chunk(near, part, delta),
            core_send.at[at], core_recv.at[at], other,
        )
        copy.start()
        core_copies[part, delta] = copy

    def keep(part, delta):
        gather(home, part, delta, core)
        core_copies[part, delta].wait_recv()
        mine, theirs = chunk(home, part, delta), chunk(near, part, delta)
        mine[...] = theirs[...] + core_sign * mine[...]
        if delta:
            at = part * 3 + delta - 1
            size = 16 * PARTS[part][1]
            copy = send(
                mine, land1[part].at[pl.ds((delta - 1) * size, size)],
                s1.at[at], r1.at[at], peer(ORDERS[part][0], delta),
            )
            copy.start()
            copies1[part, delta] = copy

    give(*sequence[0])
    for at, step in enumerate(sequence):
        if at + 1 < len(sequence):
            give(*sequence[at + 1])
        keep(*step)

    def reduced(own, landed, size, axis, start, count):
        here = place[axis]
        total = parity_sign(here, 2) * own[pl.ds(start, count), :]
        for delta in range(1, 4):
            sign = parity_sign(here & (here ^ delta), 2)
            total = total + sign * landed[pl.ds((delta - 1) * size + start, count), :]
        return total

    copies2 = {}
    for part in range(3):
        count = PARTS[part][1]
        for delta in range(1, 4):
            copies1[part, delta].wait_recv()
        for delta in (1, 2, 3, 0):
            span = pl.ds(delta * 4 * count, 4 * count)
            sum1[part][span, :] = reduced(
                home[part], land1[part], 16 * count, ORDERS[part][0], delta * 4 * count, 4 * count
            )
            if delta:
                at = part * 3 + delta - 1
                copy = send(
                    sum1[part].at[span],
                    land2[part].at[pl.ds((delta - 1) * 4 * count, 4 * count)],
                    s2.at[at], r2.at[at], peer(ORDERS[part][1], delta),
                )
                copy.start()
                copies2[part, delta] = copy

    copies3 = {}
    for part in range(3):
        count = PARTS[part][1]
        for delta in range(1, 4):
            copies2[part, delta].wait_recv()
        for delta in (1, 2, 3, 0):
            span = pl.ds(delta * count, count)
            sum2[part][span, :] = reduced(
                sum1[part], land2[part], 4 * count, ORDERS[part][1], delta * count, count
            )
            if delta:
                at = part * 3 + delta - 1
                copy = send(
                    sum2[part].at[span], land3[part].at[pl.ds((delta - 1) * count, count)],
                    s3.at[at], r3.at[at], peer(ORDERS[part][2], delta),
                )
                copy.start()
                copies3[part, delta] = copy

    for part in range(3):
        offset, count = PARTS[part]
        for delta in range(1, 4):
            copies3[part, delta].wait_recv()
        sketch[pl.ds(offset, count), :] = scale * reduced(
            sum2[part], land3[part], count, ORDERS[part][2], 0, count
        )

    rows_here = jnp.concatenate(
        [sketch[...], jnp.zeros((COLS - samples, COLS), jnp.float32)], axis=0
    )
    turned = jnp.transpose(rows_here)
    device_total = lax.axis_size("hi") * lax.axis_size("lo")
    gram[0] = jnp.dot(
        turned, rows_here, precision=lax.Precision.HIGHEST, preferred_element_type=jnp.float32
    ) * (1.0 / (samples * device_total))

    core_gram = send(gram.at[0], core_land, gcs, gcr, other)
    core_gram.start()
    core_gram.wait_recv()
    gram[1] = gram[0] + core_land[...]
    gram_copies = []
    for stage in range(3):
        now = {}
        for part in range(3):
            offset, count = GRAM_PARTS[part]
            span = pl.ds(offset, count)
            for delta in range(1, 4):
                at = stage * 9 + part * 3 + delta - 1
                copy = send(
                    gram.at[stage + 1, span], gram_land.at[stage * 3 + delta - 1, span],
                    gs.at[at], gr.at[at], peer(ORDERS[part][stage], delta),
                )
                copy.start()
                now[part, delta] = copy
                gram_copies.append(copy)
        for part in range(3):
            offset, count = GRAM_PARTS[part]
            span = pl.ds(offset, count)
            for delta in range(1, 4):
                now[part, delta].wait_recv()
            own = gram[stage + 1, span, :]
            one, two, three = (gram_land[stage * 3 + d, span, :] for d in range(3))
            gram[stage + 2, span, :] = (own + two) + (one + three)

    def put(base, value):
        augmented[base : base + BLOCK, :] = value

    eliminate(jnp.concatenate([gram[4], turned], axis=1), put)
    row_at = lax.broadcasted_iota(jnp.int32, (COLS, COLS), 0)
    col_at = lax.broadcasted_iota(jnp.int32, (COLS, COLS), 1)
    r_ref[...] = jnp.where(row_at <= col_at, augmented[:, :COLS], 0.0)
    q_ref[...] = jnp.transpose(augmented[:, COLS:])[:samples, :]

    for group in (core_copies, copies1, copies2, copies3):
        for copy in group.values():
            copy.wait_send()
    core_gram.wait_send()
    for copy in gram_copies:
        copy.wait_send()


def shards(panel, signs, sample_rows):
    rows, cols = panel.shape
    devices = lax.axis_size(("hi", "lo"))
    samples = sample_rows.shape[0] // devices
    counts = [count for _, count in PARTS]
    f32 = jnp.float32

    def buffers(blocks):
        return [pltpu.VMEM((blocks * count, cols), f32) for count in counts]

    dma = pltpu.SemaphoreType.DMA
    vmem = pl.BlockSpec(memory_space=pltpu.VMEM)
    hbm = pl.BlockSpec(memory_space=pltpu.HBM)
    return pl.pallas_call(
        functools.partial(kernel, 1.0 / math.sqrt(rows * devices), samples),
        out_shape=(
            jax.ShapeDtypeStruct((samples, cols), f32),
            jax.ShapeDtypeStruct((cols, cols), f32),
        ),
        in_specs=[hbm, hbm, hbm],
        out_specs=(vmem, vmem),
        scratch_shapes=[
            pltpu.VMEM((rows, cols), f32),
            pltpu.VMEM((rows, cols), f32),
            pltpu.VMEM((MIX, MIX), jnp.bfloat16),
            pltpu.VMEM((rows // COLS, COLS), jnp.int32),
            pltpu.SMEM(sample_rows.shape, jnp.int32),
            buffers(64), buffers(64), buffers(64),
            buffers(48), buffers(16), buffers(12), buffers(4), buffers(3),
            pltpu.VMEM((samples, cols), f32),
            pltpu.VMEM((5, cols, cols), f32),
            pltpu.VMEM((9, cols, cols), f32),
            pltpu.VMEM((cols, cols), f32),
            pltpu.VMEM((cols, 2 * cols), f32),
            dma((LOADS,)), dma, dma, dma((12,)), dma((12,)),
            dma((9,)), dma((9,)), dma((9,)), dma((9,)), dma((9,)), dma((9,)),
            dma((27,)), dma((27,)), dma, dma,
        ],
        compiler_params=pltpu.CompilerParams(
            collective_id=0, has_side_effects=True, vmem_limit_bytes=63 * 2**20
        ),
        name="sketch_qr",
    )(panel, signs.reshape(rows // COLS, COLS), sample_rows)


def solution(mesh):
    placed = (P(("hi", "lo"), None), P(("hi", "lo")), P())
    return jax.shard_map(
        shards, mesh=mesh, in_specs=placed, out_specs=(P(("hi", "lo"), None), P()), check_vma=False
    )
```

```python
import functools
import math

import jax
import jax.numpy as jnp
from jax import lax
from jax.experimental import pallas as pl
from jax.experimental.pallas import tpu as pltpu
from jax.sharding import PartitionSpec as P

MESH = pl.DeviceIdType.MESH
COLS = 128
MIX = 128
LOADS = 8
BLOCK = 16
PART = 24
GRAM_PART = 48
DELTAS = 0x36
AHEAD = 3


def parity_sign(value, bits):
    total = value & 1
    for place in range(1, bits):
        total = total + ((value >> place) & 1)
    return 1.0 - 2.0 * (total & 1).astype(jnp.float32)


def hadamard(order):
    shape = (order, order)
    common = lax.broadcasted_iota(jnp.int32, shape, 0) & lax.broadcasted_iota(jnp.int32, shape, 1)
    return parity_sign(common, order.bit_length() - 1)


def butterfly(values):
    half = 1
    values = list(values)
    while half < len(values):
        for at in range(len(values)):
            if at & half == 0:
                low, high = values[at], values[at + half]
                values[at], values[at + half] = low + high, low - high
        half *= 2
    return values


def split_three(value):
    first = value.astype(jnp.bfloat16).astype(jnp.float32)
    rest = value - first
    second = rest.astype(jnp.bfloat16).astype(jnp.float32)
    return first, second, rest - second


def widen(value, width):
    return jnp.concatenate([value] * (width // COLS), axis=1)


def eliminate(rest, put):
    order, width = rest.shape
    row_at = lax.broadcasted_iota(jnp.int32, (BLOCK, COLS), 0)
    for step in range(order // BLOCK):
        base = step * BLOCK
        rows = rest[:BLOCK]
        columns = [
            jnp.broadcast_to(rows[:, base + m : base + m + 1], (BLOCK, COLS)) for m in range(BLOCK)
        ]
        pivots = jnp.ones((BLOCK, COLS), jnp.float32)
        for j in range(BLOCK):
            pivot = jnp.broadcast_to(columns[j][j : j + 1, :], (BLOCK, COLS))
            pivots = jnp.where(row_at == j, pivot, pivots)
            if j < BLOCK - 1:
                factor = jnp.where(row_at > j, columns[j] * (1.0 / pivot), 0.0)
                for m in range(j + 1, BLOCK):
                    columns[m] = columns[m] - factor * jnp.broadcast_to(
                        columns[m][j : j + 1, :], (BLOCK, COLS)
                    )
                rows = rows - widen(factor, width) * jnp.broadcast_to(
                    rows[j : j + 1, :], (BLOCK, width)
                )
        done = rows * widen(lax.rsqrt(pivots), width)
        put(base, done)
        if base + BLOCK < order:
            a, b, c = split_three(done)
            left = jnp.concatenate([t[:, :COLS] for t in (a, a, a, b, b, c)], axis=0)
            right = jnp.concatenate([a, b, c, a, b, a], axis=0).astype(jnp.bfloat16)
            turned = jnp.transpose(left)[base + BLOCK :, :].astype(jnp.bfloat16)
            rest = rest[BLOCK:] - jnp.dot(turned, right, preferred_element_type=jnp.float32)


def kernel(
    scale, samples, panel_hbm, sign_hbm, index_hbm, q_ref, r_ref,
    panel, work, mix, sign_ref, index_rows, index, away, near, home, land1, sum1, land2, sum2, land3, sketch,
    gram, gram_land, core_land, augmented,
    load_sem, sign_sem, index_sem, core_send, core_recv, s1, r1, s2, r2, s3, r3, gs, gr, gcs, gcr,
):
    core = lax.axis_index("lo") % 2
    chip = lax.axis_index("hi") * 4 + lax.axis_index("lo") // 2
    rows = panel.shape[0]

    def device(which_chip, which_core):
        return (which_chip // 4, (which_chip % 4) * 2 + which_core)

    def shift(part, level):
        return 4 - 2 * ((part + level) % 3)

    def peer(part, level, delta):
        return device(chip ^ (delta << shift(part, level)), core)

    def sign(part, level, delta):
        here = (chip >> shift(part, level)) & 3
        return parity_sign(here & (here ^ delta), 2)

    def split_step(step):
        return step % 3, (DELTAS >> (2 * (step // 3))) & 3

    def block(ref, at, count):
        return ref.at[pl.ds(pl.multiple_of(at * count, 8), count)]

    other = device(chip, 1 - core)
    barrier = pltpu.get_barrier_semaphore()
    pl.semaphore_signal(barrier, inc=1, device_id=other, device_id_type=MESH)

    def greet(step, carry):
        pl.semaphore_signal(
            barrier, inc=1, device_id=peer(step % 3, 0, step // 3 + 1), device_id_type=MESH
        )
        return carry

    lax.fori_loop(0, 9, greet, 0)

    outer = rows // MIX
    per_load = outer // LOADS
    piece = rows // LOADS

    def load(at):
        span = pl.ds(pl.multiple_of(at * piece, piece), piece)
        return pltpu.make_async_copy(panel_hbm.at[span], panel.at[span], load_sem.at[at])

    sign_copy = pltpu.make_async_copy(sign_hbm, sign_ref, sign_sem)
    sign_copy.start()
    for at in range(LOADS):
        load(at).start()
    index_copy = pltpu.make_async_copy(index_hbm, index_rows, index_sem)
    index_copy.start()
    mix[...] = hadamard(MIX).astype(jnp.bfloat16)
    sign_copy.wait()

    def mix_group(at, carry):
        load(at).wait()
        for inner in range(per_load):
            line = at * per_load + inner
            start = pl.multiple_of(line * MIX, MIX)
            value = panel[pl.ds(start, MIX), :]
            high = value.astype(jnp.bfloat16)
            low = (value - high.astype(jnp.float32)).astype(jnp.bfloat16)
            signs = sign_ref[pl.ds(line, 1), :].astype(jnp.float32)
            signed_mix = mix[...] * jnp.broadcast_to(signs, (MIX, MIX)).astype(jnp.bfloat16)
            work[pl.ds(start, MIX), :] = jnp.dot(
                jnp.concatenate([signed_mix, signed_mix], axis=1),
                jnp.concatenate([high, low], axis=0),
                preferred_element_type=jnp.float32,
            )
        return carry

    lax.fori_loop(0, LOADS, mix_group, 0)
    index_copy.wait()
    index_rows[...] = index_rows[...] & (rows - 1)
    index_move = pltpu.make_async_copy(index_rows, index, index_sem)
    index_move.start()

    def butterflies(order, outer_stride, stride, unroll):
        def group(at, carry):
            def tile(t, carry):
                base = pl.multiple_of(at * outer_stride + t * 8, 8)
                spans = [pl.ds(pl.multiple_of(base + m * stride, 8), 8) for m in range(order)]
                for span, value in zip(spans, butterfly([work[span, :] for span in spans])):
                    work[span, :] = value
                return carry

            return lax.fori_loop(0, MIX // 8, tile, carry, unroll=unroll)

        lax.fori_loop(0, outer // order, group, 0)

    butterflies(per_load, per_load * MIX, MIX, 2)
    butterflies(LOADS, MIX, per_load * MIX, 4)
    index_move.wait()

    def gather(step, which, write):
        part, delta = split_step(step)
        count = min(PART, samples - part * PART)

        def one(j, carry):
            for inner in range(4):
                to_chip = chip ^ (
                    (delta << shift(part, 0)) | (j << shift(part, 1)) | (inner << shift(part, 2))
                )
                base = (to_chip * 2 + which) * samples + part * PART
                to = pl.multiple_of(step * 16 * PART + (j * 4 + inner) * PART, 8)
                for k in range(count):
                    write(to + k, work[pl.ds(index[base + k], 1), :])
            return carry

        lax.fori_loop(0, 4, one, 0)

    def send(source, target, send_sem, recv_sem, to):
        return pltpu.make_async_remote_copy(
            src_ref=source, dst_ref=target, send_sem=send_sem, recv_sem=recv_sem,
            device_id=to, device_id_type=MESH,
        )

    def core_copy(step):
        return send(
            block(away, step, 16 * PART), block(near, step, 16 * PART),
            core_send.at[step], core_recv.at[step], other,
        )

    def part_copy(source, target, count, sends, recvs, level, step):
        part, delta = split_step(step)
        return send(
            block(source, step, count), block(target, step, count),
            sends.at[step], recvs.at[step], peer(part, level, delta),
        )

    copy1 = functools.partial(part_copy, home, land1, 16 * PART, s1, r1, 0)
    copy2 = functools.partial(part_copy, sum1, land2, 4 * PART, s2, r2, 1)
    copy3 = functools.partial(part_copy, sum2, land3, PART, s3, r3, 2)
    core_sign = 1.0 - 2.0 * core.astype(jnp.float32)

    def write_away(to, value):
        away[pl.ds(to, 1), :] = value

    def write_home(to, value):
        home[pl.ds(to, 1), :] = near[pl.ds(to, 1), :] + core_sign * value

    pl.semaphore_wait(barrier, 10)

    for at in range(12 + AHEAD):
        if at < 12:
            gather(at, 1 - core, write_away)
            core_copy(at).start()
        if at >= AHEAD:
            step = at - AHEAD
            core_copy(step).wait_recv()
            gather(step, core, write_home)
            if step < 9:
                copy1(step).start()

    def total(own, landed, part, level, own_at, land_at, land_stride):
        out = sign(part, level, 0) * own[pl.ds(own_at, 8), :]
        for hop in range(3):
            delta = (DELTAS >> (2 * hop)) & 3
            at = pl.multiple_of(land_at + hop * land_stride, 8)
            out = out + sign(part, level, delta) * landed[pl.ds(at, 8), :]
        return out

    def fold(own, landed, count, level, copy_in, target, copy_out):
        whole = 4 * count

        def one(step, carry):
            part, delta = split_step(step)

            @pl.when(step < 3)
            def _():
                for hop in range(3):
                    copy_in(hop * 3 + part).wait_recv()

            def tile(t, carry):
                inside = delta * count + t * 8
                target[pl.ds(pl.multiple_of(step * count + t * 8, 8), 8), :] = total(
                    own, landed, part, level,
                    pl.multiple_of((9 + part) * whole + inside, 8), part * whole + inside, 3 * whole,
                )
                return carry

            lax.fori_loop(0, count // 8, tile, 0, unroll=3)

            @pl.when(step < 9)
            def _():
                copy_out(step).start()

            return carry

        lax.fori_loop(0, 12, one, 0)

    fold(home, land1, 4 * PART, 0, copy1, sum1, copy2)
    fold(sum1, land2, PART, 1, copy2, sum2, copy3)

    def finish(part, carry):
        for hop in range(3):
            copy3(hop * 3 + part).wait_recv()
        for t in range(PART // 8):
            inside = part * PART + t * 8
            sketch[pl.ds(pl.multiple_of(inside, 8), 8), :] = scale * total(
                sum2, land3, part, 2, pl.multiple_of(9 * PART + inside, 8), inside, 3 * PART
            )
        return carry

    lax.fori_loop(0, 3, finish, 0)

    rows_here = jnp.concatenate(
        [sketch[:samples, :], jnp.zeros((COLS - samples, COLS), jnp.float32)], axis=0
    )
    turned = jnp.transpose(rows_here)
    device_total = lax.axis_size("hi") * lax.axis_size("lo")
    gram[0, :COLS, :] = jnp.dot(
        turned, rows_here, precision=lax.Precision.HIGHEST, preferred_element_type=jnp.float32
    ) * (1.0 / (samples * device_total))
    gram[0, COLS:, :] = jnp.zeros((3 * GRAM_PART - COLS, COLS), jnp.float32)

    core_gram = send(gram.at[0], core_land, gcs, gcr, other)
    core_gram.start()
    core_gram.wait_recv()
    gram[1] = gram[0] + core_land[...]

    def gram_copy(stage, step):
        part, delta = split_step(step)
        span = pl.ds(pl.multiple_of(part * GRAM_PART, 8), GRAM_PART)
        at = stage * 9 + step
        return send(
            gram.at[stage + 1, span], gram_land.at[stage * 3 + step // 3, span],
            gs.at[at], gr.at[at], peer(part, stage, delta),
        )

    def gram_stage(stage, carry):
        def start(step, carry):
            gram_copy(stage, step).start()
            return carry

        lax.fori_loop(0, 9, start, 0)

        def add(part, carry):
            for hop in range(3):
                gram_copy(stage, hop * 3 + part).wait_recv()
            for t in range(GRAM_PART // 8):
                span = pl.ds(pl.multiple_of(part * GRAM_PART + t * 8, 8), 8)
                own = gram[stage + 1, span, :]
                two, one, three = (gram_land[stage * 3 + hop, span, :] for hop in range(3))
                gram[stage + 2, span, :] = (own + two) + (one + three)
            return carry

        return lax.fori_loop(0, 3, add, carry)

    lax.fori_loop(0, 3, gram_stage, 0)

    def put(base, value):
        augmented[base : base + BLOCK, :] = value

    eliminate(jnp.concatenate([gram[4, :COLS, :], turned], axis=1), put)
    row_at = lax.broadcasted_iota(jnp.int32, (COLS, COLS), 0)
    col_at = lax.broadcasted_iota(jnp.int32, (COLS, COLS), 1)
    r_ref[...] = jnp.where(row_at <= col_at, augmented[:, :COLS], 0.0)
    q_ref[...] = jnp.transpose(augmented[:, COLS:])[:samples, :]

    def drain_core(step, carry):
        core_copy(step).wait_send()
        return carry

    def drain(step, carry):
        for copy in (copy1, copy2, copy3):
            copy(step).wait_send()
        for stage in range(3):
            gram_copy(stage, step).wait_send()
        return carry

    lax.fori_loop(0, 12, drain_core, 0)
    lax.fori_loop(0, 9, drain, 0)
    core_gram.wait_send()


def shards(panel, signs, sample_rows):
    rows, cols = panel.shape
    devices = lax.axis_size(("hi", "lo"))
    samples = sample_rows.shape[0] // devices
    f32 = jnp.float32

    def buffers(blocks):
        return pltpu.VMEM((blocks * 3 * PART, cols), f32)

    dma = pltpu.SemaphoreType.DMA
    vmem = pl.BlockSpec(memory_space=pltpu.VMEM)
    hbm = pl.BlockSpec(memory_space=pltpu.HBM)
    return pl.pallas_call(
        functools.partial(kernel, 1.0 / math.sqrt(rows * devices), samples),
        out_shape=(
            pltpu.VMEM((samples, cols), f32),
            pltpu.VMEM((cols, cols), f32),
        ),
        in_specs=[hbm, hbm, hbm],
        out_specs=(vmem, vmem),
        scratch_shapes=[
            pltpu.VMEM((rows, cols), f32),
            pltpu.VMEM((rows, cols), f32),
            pltpu.VMEM((MIX, MIX), jnp.bfloat16),
            pltpu.VMEM((rows // COLS, COLS), jnp.int32),
            pltpu.VMEM(sample_rows.shape, jnp.int32),
            pltpu.SMEM(sample_rows.shape, jnp.int32),
            buffers(64), buffers(64), buffers(64),
            buffers(48), buffers(16), buffers(12), buffers(4), buffers(3),
            pltpu.VMEM((3 * PART, cols), f32),
            pltpu.VMEM((5, 3 * GRAM_PART, cols), f32),
            pltpu.VMEM((9, 3 * GRAM_PART, cols), f32),
            pltpu.VMEM((3 * GRAM_PART, cols), f32),
            pltpu.VMEM((cols, 2 * cols), f32),
            dma((LOADS,)), dma, dma, dma((12,)), dma((12,)),
            dma((9,)), dma((9,)), dma((9,)), dma((9,)), dma((9,)), dma((9,)),
            dma((27,)), dma((27,)), dma, dma,
        ],
        compiler_params=pltpu.CompilerParams(
            collective_id=0, has_side_effects=True, vmem_limit_bytes=63 * 2**20
        ),
        name="sketch_qr",
    )(panel, signs.reshape(rows // COLS, COLS), sample_rows)


def solution(mesh):
    placed = (P(("hi", "lo"), None), P(("hi", "lo")), P())
    return jax.shard_map(
        shards, mesh=mesh, in_specs=placed, out_specs=(P(("hi", "lo"), None), P()), check_vma=False
    )
```

```python
import functools
import math

import jax
import jax.numpy as jnp
from jax import lax
from jax.experimental import pallas as pl
from jax.experimental.pallas import tpu as pltpu
from jax.sharding import PartitionSpec as P

MESH = pl.DeviceIdType.MESH
COLS = 128
MIX = 128
LOADS = 8
BLOCK = 16
PART = 24
GRAM_PART = 32
IN_FLIGHT = 4
PIECES = 2
DELTAS = 0x36
AHEAD = 3


def parity_sign(value, bits):
    total = value & 1
    for place in range(1, bits):
        total = total + ((value >> place) & 1)
    return 1.0 - 2.0 * (total & 1).astype(jnp.float32)


def hadamard(order):
    shape = (order, order)
    common = lax.broadcasted_iota(jnp.int32, shape, 0) & lax.broadcasted_iota(jnp.int32, shape, 1)
    return parity_sign(common, order.bit_length() - 1)


def butterfly(values):
    half = 1
    values = list(values)
    while half < len(values):
        for at in range(len(values)):
            if at & half == 0:
                low, high = values[at], values[at + half]
                values[at], values[at + half] = low + high, low - high
        half *= 2
    return values


def split_three(value):
    first = value.astype(jnp.bfloat16).astype(jnp.float32)
    rest = value - first
    second = rest.astype(jnp.bfloat16).astype(jnp.float32)
    return first, second, rest - second


def widen(value, width):
    return jnp.concatenate([value] * (width // COLS), axis=1)


def eliminate(rest, put):
    order, width = rest.shape
    row_at = lax.broadcasted_iota(jnp.int32, (BLOCK, COLS), 0)
    for step in range(order // BLOCK):
        base = step * BLOCK
        rows = rest[:BLOCK]
        columns = [
            jnp.broadcast_to(rows[:, base + m : base + m + 1], (BLOCK, COLS)) for m in range(BLOCK)
        ]
        pivots = jnp.ones((BLOCK, COLS), jnp.float32)
        for j in range(BLOCK):
            pivot = jnp.broadcast_to(columns[j][j : j + 1, :], (BLOCK, COLS))
            pivots = jnp.where(row_at == j, pivot, pivots)
            if j < BLOCK - 1:
                factor = jnp.where(row_at > j, columns[j] * (1.0 / pivot), 0.0)
                for m in range(j + 1, BLOCK):
                    columns[m] = columns[m] - factor * jnp.broadcast_to(
                        columns[m][j : j + 1, :], (BLOCK, COLS)
                    )
                rows = rows - widen(factor, width) * jnp.broadcast_to(
                    rows[j : j + 1, :], (BLOCK, width)
                )
        done = rows * widen(lax.rsqrt(pivots), width)
        put(base, done)
        if base + BLOCK < order:
            a, b, c = split_three(done)
            left = jnp.concatenate([t[:, :COLS] for t in (a, a, a, b, b, c)], axis=0)
            right = jnp.concatenate([a, b, c, a, b, a], axis=0).astype(jnp.bfloat16)
            turned = jnp.transpose(left)[base + BLOCK :, :].astype(jnp.bfloat16)
            rest = rest[BLOCK:] - jnp.dot(turned, right, preferred_element_type=jnp.float32)


def kernel(
    scale, samples, panel_hbm, sign_hbm, index_hbm, q_ref, r_ref,
    panel, work, mix, sign_ref, index_rows, index, away, near, home, land1, sum1, land2, sum2, land3, sketch,
    gram, gram_land, core_land, augmented,
    load_sem, sign_sem, index_sem, core_send, core_recv, s1, r1, s2, r2, s3, r3, gs, gr, gcs, gcr,
):
    core = lax.axis_index("lo") % 2
    chip = lax.axis_index("hi") * 4 + lax.axis_index("lo") // 2
    rows = panel.shape[0]

    def device(which_chip, which_core):
        return (which_chip // 4, (which_chip % 4) * 2 + which_core)

    def shift(part, level):
        axis = part + level
        return 4 - 2 * (axis % 3) if isinstance(axis, int) else 4 - 2 * lax.rem(axis, 3)

    def peer(part, level, delta):
        return device(chip ^ (delta << shift(part, level)), core)

    def sign(part, level, delta):
        here = (chip >> shift(part, level)) & 3
        return parity_sign(here & (here ^ delta), 2)

    def split_step(step):
        return step % 3, (DELTAS >> (2 * (step // 3))) & 3

    def block(ref, at, count):
        return ref.at[pl.ds(at * count if isinstance(at, int) else pl.multiple_of(at * count, 8), count)]

    other = device(chip, 1 - core)
    barrier = pltpu.get_barrier_semaphore()
    pl.semaphore_signal(barrier, inc=1, device_id=other, device_id_type=MESH)

    def greet(step, carry):
        pl.semaphore_signal(
            barrier, inc=1, device_id=peer(step % 3, 0, step // 3 + 1), device_id_type=MESH
        )
        return carry

    lax.fori_loop(0, 9, greet, 0)

    outer = rows // MIX
    per_load = outer // LOADS
    piece = rows // LOADS

    def load(at):
        span = pl.ds(pl.multiple_of(at * piece, piece), piece)
        return pltpu.make_async_copy(panel_hbm.at[span], panel.at[span], load_sem.at[at])

    sign_copy = pltpu.make_async_copy(sign_hbm, sign_ref, sign_sem)
    sign_copy.start()
    for at in range(IN_FLIGHT):
        load(at).start()
    index_copy = pltpu.make_async_copy(index_hbm, index_rows, index_sem)
    index_copy.start()
    mix[...] = hadamard(MIX).astype(jnp.bfloat16)
    sign_copy.wait()

    def mix_group(at, carry):
        load(at).wait()

        @pl.when(at + IN_FLIGHT < LOADS)
        def _():
            load(at + IN_FLIGHT).start()

        for inner in range(per_load):
            line = at * per_load + inner
            start = pl.multiple_of(line * MIX, MIX)
            value = panel[pl.ds(start, MIX), :]
            high = value.astype(jnp.bfloat16)
            low = (value - high.astype(jnp.float32)).astype(jnp.bfloat16)
            signs = sign_ref[pl.ds(line, 1), :].astype(jnp.float32)
            signed_mix = mix[...] * jnp.broadcast_to(signs, (MIX, MIX)).astype(jnp.bfloat16)
            work[pl.ds(start, MIX), :] = jnp.dot(
                jnp.concatenate([signed_mix, signed_mix], axis=1),
                jnp.concatenate([high, low], axis=0),
                preferred_element_type=jnp.float32,
            )
        return carry

    lax.fori_loop(0, LOADS, mix_group, 0)
    index_copy.wait()
    index_rows[...] = index_rows[...] & (rows - 1)
    index_move = pltpu.make_async_copy(index_rows, index, index_sem)
    index_move.start()

    def butterflies(order, outer_stride, stride, unroll):
        def group(at, carry):
            def tile(t, carry):
                base = pl.multiple_of(at * outer_stride + t * 8, 8)
                spans = [pl.ds(pl.multiple_of(base + m * stride, 8), 8) for m in range(order)]
                for span, value in zip(spans, butterfly([work[span, :] for span in spans])):
                    work[span, :] = value
                return carry

            return lax.fori_loop(0, MIX // 8, tile, carry, unroll=unroll)

        lax.fori_loop(0, outer // order, group, 0)

    butterflies(per_load, per_load * MIX, MIX, 2)
    butterflies(LOADS, MIX, per_load * MIX, 4)
    index_move.wait()

    def gather(step, cut, which, write):
        part, delta = split_step(step)
        count = min(PART, samples - part * PART)

        def one(j, carry):
            for inner in range(4):
                to_chip = chip ^ (
                    (delta << shift(part, 0)) | (j << shift(part, 1)) | (inner << shift(part, 2))
                )
                base = (to_chip * 2 + which) * samples + part * PART
                to = pl.multiple_of(step * 16 * PART + (j * 4 + inner) * PART, 8)
                for k in range(count):
                    write(to + k, work[pl.ds(index[base + k], 1), :])
            return carry

        lax.fori_loop(cut * 4 // PIECES, (cut + 1) * 4 // PIECES, one, 0)

    def send(source, target, send_sem, recv_sem, to):
        return pltpu.make_async_remote_copy(
            src_ref=source, dst_ref=target, send_sem=send_sem, recv_sem=recv_sem,
            device_id=to, device_id_type=MESH,
        )

    def core_copy(step, cut):
        at, size = step * PIECES + cut, 16 * PART // PIECES
        return send(
            block(away, at, size), block(near, at, size),
            core_send.at[at], core_recv.at[at], other,
        )

    def copy1(step, cut):
        part, delta = split_step(step)
        at, size = step * PIECES + cut, 16 * PART // PIECES
        return send(
            block(home, at, size), block(land1, at, size),
            s1.at[at], r1.at[at], peer(part, 0, delta),
        )

    def part_copy(source, target, count, sends, recvs, level, step):
        part, delta = split_step(step)
        return send(
            block(source, step, count), block(target, step, count),
            sends.at[step], recvs.at[step], peer(part, level, delta),
        )

    copy2 = functools.partial(part_copy, sum1, land2, 4 * PART, s2, r2, 1)
    copy3 = functools.partial(part_copy, sum2, land3, PART, s3, r3, 2)
    core_sign = 1.0 - 2.0 * core.astype(jnp.float32)

    def write_away(to, value):
        away[pl.ds(to, 1), :] = value

    def write_home(to, value):
        home[pl.ds(to, 1), :] = near[pl.ds(to, 1), :] + core_sign * value

    pl.semaphore_wait(barrier, 10)

    order = [(hop * 3 + part, cut) for cut in range(PIECES) for hop in range(3) for part in range(3)]
    order += [(9 + part, cut) for part in range(3) for cut in range(PIECES)]
    for at in range(len(order) + AHEAD):
        if at < len(order):
            gather(*order[at], 1 - core, write_away)
            core_copy(*order[at]).start()
        if at >= AHEAD:
            step, cut = order[at - AHEAD]
            core_copy(step, cut).wait_recv()
            gather(step, cut, core, write_home)
            if step < 9:
                copy1(step, cut).start()

    def total(own, landed, part, level, own_at, land_at, land_stride):
        out = sign(part, level, 0) * own[pl.ds(own_at, 8), :]
        for hop in range(3):
            delta = (DELTAS >> (2 * hop)) & 3
            at = land_at + hop * land_stride
            out = out + sign(part, level, delta) * landed[pl.ds(at, 8), :]
        return out

    def fold(own, landed, count, level, copy_in, target, copy_out):
        whole = 4 * count

        for part in range(3):
            for hop in range(3):
                copy_in(hop * 3 + part)
        for step in range(12):
            part, delta = split_step(step)

            for t in range(count // 8):
                inside = delta * count + t * 8
                target[pl.ds(step * count + t * 8, 8), :] = total(
                    own, landed, part, level,
                    (9 + part) * whole + inside, part * whole + inside, 3 * whole,
                )
            if step < 9:
                copy_out(step).start()

    def landed1(step):
        for cut in range(PIECES):
            copy1(step, cut).wait_recv()

    fold(home, land1, 4 * PART, 0, landed1, sum1, copy2)
    fold(sum1, land2, PART, 1, lambda step: copy2(step).wait_recv(), sum2, copy3)

    for part in range(3):
        for hop in range(3):
            copy3(hop * 3 + part).wait_recv()
        for t in range(PART // 8):
            inside = part * PART + t * 8
            sketch[pl.ds(inside, 8), :] = scale * total(
                sum2, land3, part, 2, 9 * PART + inside, inside, 3 * PART
            )

    rows_here = jnp.concatenate(
        [sketch[:samples, :], jnp.zeros((COLS - samples, COLS), jnp.float32)], axis=0
    )
    turned = jnp.transpose(rows_here)
    device_total = lax.axis_size("hi") * lax.axis_size("lo")
    local = jnp.dot(
        turned, rows_here, precision=lax.Precision.HIGHEST, preferred_element_type=jnp.float32
    ) * (1.0 / (samples * device_total))
    half, quarter = COLS // 2, COLS // 4
    left_half = lax.broadcasted_iota(jnp.int32, (quarter, COLS), 1) < half
    gram[0, :half, :] = local[:half]
    gram[0, half:, :] = jnp.where(
        left_half, pltpu.roll(local[half : half + quarter], half, 1), local[half + quarter :]
    )

    core_gram = send(gram.at[0], core_land, gcs, gcr, other)
    core_gram.start()
    core_gram.wait_recv()
    gram[1] = gram[0] + core_land[...]

    def gram_copy(stage, step):
        part, delta = split_step(step)
        at = stage * 9 + step
        return send(
            block(gram.at[stage + 1], part, GRAM_PART),
            block(gram_land.at[stage * 3 + step // 3], part, GRAM_PART),
            gs.at[at], gr.at[at], peer(part, stage, delta),
        )

    for stage in range(3):
        for step in range(9):
            gram_copy(stage, step).start()
        for part in range(3):
            for hop in range(3):
                gram_copy(stage, hop * 3 + part).wait_recv()
            span = pl.ds(part * GRAM_PART, GRAM_PART)
            own = gram[stage + 1, span, :]
            two, one, three = (gram_land[stage * 3 + hop, span, :] for hop in range(3))
            gram[stage + 2, span, :] = (own + two) + (one + three)

    def put(base, value):
        augmented[base : base + BLOCK, :] = value

    packed = gram[4, half:, :]
    whole_gram = jnp.concatenate(
        [gram[4, :half, :], pltpu.roll(packed, half, 1), packed], axis=0
    )
    eliminate(jnp.concatenate([whole_gram, turned], axis=1), put)
    row_at = lax.broadcasted_iota(jnp.int32, (COLS, COLS), 0)
    col_at = lax.broadcasted_iota(jnp.int32, (COLS, COLS), 1)
    r_ref[...] = jnp.where(row_at <= col_at, augmented[:, :COLS], 0.0)
    q_ref[...] = jnp.transpose(augmented[:, COLS:])[:samples, :]

    for step, cut in order:
        core_copy(step, cut).wait_send()
        if step < 9:
            copy1(step, cut).wait_send()
    for step in range(9):
        for copy in (copy2, copy3):
            copy(step).wait_send()
        for stage in range(3):
            gram_copy(stage, step).wait_send()
    core_gram.wait_send()


def shards(panel, signs, sample_rows):
    rows, cols = panel.shape
    devices = lax.axis_size(("hi", "lo"))
    samples = sample_rows.shape[0] // devices
    f32 = jnp.float32

    def buffers(blocks):
        return pltpu.VMEM((blocks * 3 * PART, cols), f32)

    dma = pltpu.SemaphoreType.DMA
    vmem = pl.BlockSpec(memory_space=pltpu.VMEM)
    hbm = pl.BlockSpec(memory_space=pltpu.HBM)
    return pl.pallas_call(
        functools.partial(kernel, 1.0 / math.sqrt(rows * devices), samples),
        out_shape=(
            pltpu.VMEM((samples, cols), f32),
            pltpu.VMEM((cols, cols), f32),
        ),
        in_specs=[hbm, hbm, hbm],
        out_specs=(vmem, vmem),
        scratch_shapes=[
            pltpu.VMEM((rows, cols), f32),
            pltpu.VMEM((rows, cols), f32),
            pltpu.VMEM((MIX, MIX), jnp.bfloat16),
            pltpu.VMEM((rows // COLS, COLS), jnp.int32),
            pltpu.VMEM(sample_rows.shape, jnp.int32),
            pltpu.SMEM(sample_rows.shape, jnp.int32),
            buffers(64), buffers(64), buffers(64),
            buffers(48), buffers(16), buffers(12), buffers(4), buffers(3),
            pltpu.VMEM((3 * PART, cols), f32),
            pltpu.VMEM((5, 3 * GRAM_PART, cols), f32),
            pltpu.VMEM((9, 3 * GRAM_PART, cols), f32),
            pltpu.VMEM((3 * GRAM_PART, cols), f32),
            pltpu.VMEM((cols, 2 * cols), f32),
            dma((LOADS,)), dma, dma, dma((12 * PIECES,)), dma((12 * PIECES,)),
            dma((9 * PIECES,)), dma((9 * PIECES,)), dma((9,)), dma((9,)), dma((9,)), dma((9,)),
            dma((27,)), dma((27,)), dma, dma,
        ],
        compiler_params=pltpu.CompilerParams(
            collective_id=0, has_side_effects=True, vmem_limit_bytes=63 * 2**20
        ),
        name="sketch_qr",
    )(panel, signs.reshape(rows // COLS, COLS), sample_rows)


def solution(mesh):
    placed = (P(("hi", "lo"), None), P(("hi", "lo")), P())
    return jax.shard_map(
        shards, mesh=mesh, in_specs=placed, out_specs=(P(("hi", "lo"), None), P()), check_vma=False
    )
```

```python
import functools
import math

import jax
import jax.numpy as jnp
from jax import lax
from jax.experimental import pallas as pl
from jax.experimental.pallas import tpu as pltpu
from jax.sharding import PartitionSpec as P

MESH = pl.DeviceIdType.MESH
COLS = 128
MIX = 128
LOADS = 8
BLOCK = 16
PART = 24
GRAM_PART = 32
GATHER_UNROLL = 1
IN_FLIGHT = 4
DELTAS = 0x36
AHEAD = 6


def parity_sign(value, bits):
    total = value & 1
    for place in range(1, bits):
        total = total + ((value >> place) & 1)
    return 1.0 - 2.0 * (total & 1).astype(jnp.float32)


def hadamard(order):
    shape = (order, order)
    common = lax.broadcasted_iota(jnp.int32, shape, 0) & lax.broadcasted_iota(jnp.int32, shape, 1)
    return parity_sign(common, order.bit_length() - 1)


def butterfly(values):
    half = 1
    values = list(values)
    while half < len(values):
        for at in range(len(values)):
            if at & half == 0:
                low, high = values[at], values[at + half]
                values[at], values[at + half] = low + high, low - high
        half *= 2
    return values


def split_three(value):
    first = value.astype(jnp.bfloat16).astype(jnp.float32)
    rest = value - first
    second = rest.astype(jnp.bfloat16).astype(jnp.float32)
    return first, second, rest - second


def widen(value, width):
    return jnp.concatenate([value] * (width // COLS), axis=1)


def eliminate(rest, put):
    order, width = rest.shape
    row_at = lax.broadcasted_iota(jnp.int32, (BLOCK, COLS), 0)
    for step in range(order // BLOCK):
        base = step * BLOCK
        rows = rest[:BLOCK]
        columns = [
            jnp.broadcast_to(rows[:, base + m : base + m + 1], (BLOCK, COLS)) for m in range(BLOCK)
        ]
        pivots = jnp.ones((BLOCK, COLS), jnp.float32)
        for j in range(BLOCK):
            pivot = jnp.broadcast_to(columns[j][j : j + 1, :], (BLOCK, COLS))
            pivots = jnp.where(row_at == j, pivot, pivots)
            if j < BLOCK - 1:
                factor = jnp.where(row_at > j, columns[j] * (1.0 / pivot), 0.0)
                for m in range(j + 1, BLOCK):
                    columns[m] = columns[m] - factor * jnp.broadcast_to(
                        columns[m][j : j + 1, :], (BLOCK, COLS)
                    )
                rows = rows - widen(factor, width) * jnp.broadcast_to(
                    rows[j : j + 1, :], (BLOCK, width)
                )
        done = rows * widen(lax.rsqrt(pivots), width)
        put(base, done)
        if base + BLOCK < order:
            a, b, c = split_three(done)
            left = jnp.concatenate([t[:, :COLS] for t in (a, a, a, b, b, c)], axis=0)
            right = jnp.concatenate([a, b, c, a, b, a], axis=0).astype(jnp.bfloat16)
            turned = jnp.transpose(left)[base + BLOCK :, :].astype(jnp.bfloat16)
            rest = rest[BLOCK:] - jnp.dot(turned, right, preferred_element_type=jnp.float32)


def kernel(
    scale, samples, panel_hbm, sign_hbm, index_hbm, q_ref, r_ref,
    panel, work, mix, sign_ref, index_rows, index, away, near, home, land1, sum1, land2, sum2, land3, sketch,
    gram, gram_land, core_land, augmented,
    load_sem, sign_sem, index_sem, core_send, core_recv, s1, r1, s2, r2, s3, r3, gs, gr, gcs, gcr,
):
    core = lax.axis_index("lo") % 2
    chip = lax.axis_index("hi") * 4 + lax.axis_index("lo") // 2
    rows = panel.shape[0]

    def device(which_chip, which_core):
        return (which_chip // 4, (which_chip % 4) * 2 + which_core)

    def shift(part, level):
        axis = part + level
        return 4 - 2 * (axis % 3) if isinstance(axis, int) else 4 - 2 * lax.rem(axis, 3)

    def peer(part, level, delta):
        return device(chip ^ (delta << shift(part, level)), core)

    def sign(part, level, delta):
        here = (chip >> shift(part, level)) & 3
        return parity_sign(here & (here ^ delta), 2)

    def split_step(step):
        return step % 3, (DELTAS >> (2 * (step // 3))) & 3

    def block(ref, at, count):
        return ref.at[pl.ds(at * count if isinstance(at, int) else pl.multiple_of(at * count, 8), count)]

    other = device(chip, 1 - core)
    barrier = pltpu.get_barrier_semaphore()
    pl.semaphore_signal(barrier, inc=1, device_id=other, device_id_type=MESH)

    def greet(step, carry):
        pl.semaphore_signal(
            barrier, inc=1, device_id=peer(step % 3, 0, step // 3 + 1), device_id_type=MESH
        )
        return carry

    lax.fori_loop(0, 9, greet, 0)

    outer = rows // MIX
    per_load = outer // LOADS
    piece = rows // LOADS

    def load(at):
        span = pl.ds(pl.multiple_of(at * piece, piece), piece)
        return pltpu.make_async_copy(panel_hbm.at[span], panel.at[span], load_sem.at[at])

    sign_copy = pltpu.make_async_copy(sign_hbm, sign_ref, sign_sem)
    sign_copy.start()
    for at in range(IN_FLIGHT):
        load(at).start()
    index_copy = pltpu.make_async_copy(index_hbm, index_rows, index_sem)
    index_copy.start()
    mix[...] = hadamard(MIX).astype(jnp.bfloat16)
    sign_copy.wait()

    def mix_group(at, carry):
        load(at).wait()

        @pl.when(at + IN_FLIGHT < LOADS)
        def _():
            load(at + IN_FLIGHT).start()

        for inner in range(per_load):
            line = at * per_load + inner
            start = pl.multiple_of(line * MIX, MIX)
            value = panel[pl.ds(start, MIX), :]
            high = value.astype(jnp.bfloat16)
            low = (value - high.astype(jnp.float32)).astype(jnp.bfloat16)
            signs = sign_ref[pl.ds(line, 1), :].astype(jnp.float32)
            signed_mix = mix[...] * jnp.broadcast_to(signs, (MIX, MIX)).astype(jnp.bfloat16)
            work[pl.ds(start, MIX), :] = jnp.dot(
                jnp.concatenate([signed_mix, signed_mix], axis=1),
                jnp.concatenate([high, low], axis=0),
                preferred_element_type=jnp.float32,
            )
        return carry

    lax.fori_loop(0, LOADS, mix_group, 0)
    index_copy.wait()
    index_rows[...] = index_rows[...] & (rows - 1)
    index_move = pltpu.make_async_copy(index_rows, index, index_sem)
    index_move.start()

    def butterflies(order, outer_stride, stride, unroll):
        def group(at, carry):
            def tile(t, carry):
                base = pl.multiple_of(at * outer_stride + t * 8, 8)
                spans = [pl.ds(pl.multiple_of(base + m * stride, 8), 8) for m in range(order)]
                for span, value in zip(spans, butterfly([work[span, :] for span in spans])):
                    work[span, :] = value
                return carry

            return lax.fori_loop(0, MIX // 8, tile, carry, unroll=unroll)

        lax.fori_loop(0, outer // order, group, 0)

    butterflies(per_load, per_load * MIX, MIX, 2)
    butterflies(LOADS, MIX, per_load * MIX, 4)
    index_move.wait()

    def gather(step, cut, which, write):
        part, delta = split_step(step)
        count = min(PART, samples - part * PART)

        second = (DELTAS >> (2 * cut)) & 3

        def one(third, carry):
            to_chip = chip ^ (
                (delta << shift(part, 0)) | (second << shift(part, 1)) | (third << shift(part, 2))
            )
            base = (to_chip * 2 + which) * samples + part * PART
            to = pl.multiple_of(step * 16 * PART + (second * 4 + third) * PART, 8)
            for k in range(count):
                write(to + k, work[pl.ds(index[base + k], 1), :])
            return carry

        lax.fori_loop(0, 4, one, 0, unroll=GATHER_UNROLL)

    def send(source, target, send_sem, recv_sem, to):
        return pltpu.make_async_remote_copy(
            src_ref=source, dst_ref=target, send_sem=send_sem, recv_sem=recv_sem,
            device_id=to, device_id_type=MESH,
        )

    def core_copy(step, cut):
        at, size = step * 4 + ((DELTAS >> (2 * cut)) & 3), 4 * PART
        return send(
            block(away, at, size), block(near, at, size),
            core_send.at[at], core_recv.at[at], other,
        )

    def copy1(step, cut):
        part, delta = split_step(step)
        at, size = step * 4 + ((DELTAS >> (2 * cut)) & 3), 4 * PART
        return send(
            block(home, at, size), block(land1, at, size),
            s1.at[at], r1.at[at], peer(part, 0, delta),
        )

    def part_copy(source, target, count, sends, recvs, level, step):
        part, delta = split_step(step)
        return send(
            block(source, step, count), block(target, step, count),
            sends.at[step], recvs.at[step], peer(part, level, delta),
        )

    copy2 = functools.partial(part_copy, sum1, land2, 4 * PART, s2, r2, 1)
    copy3 = functools.partial(part_copy, sum2, land3, PART, s3, r3, 2)
    core_sign = 1.0 - 2.0 * core.astype(jnp.float32)

    def write_away(to, value):
        away[pl.ds(to, 1), :] = value

    def write_home(to, value):
        home[pl.ds(to, 1), :] = near[pl.ds(to, 1), :] + core_sign * value

    pl.semaphore_wait(barrier, 10)

    order = [(hop * 3 + part, cut) for cut in range(4) for hop in range(3) for part in range(3)]
    order += [(9 + part, cut) for part in range(3) for cut in range(4)]
    for at in range(len(order) + AHEAD):
        if at < len(order):
            gather(*order[at], 1 - core, write_away)
            core_copy(*order[at]).start()
        if at >= AHEAD:
            step, cut = order[at - AHEAD]
            core_copy(step, cut).wait_recv()
            gather(step, cut, core, write_home)
            if step < 9:
                copy1(step, cut).start()

    def total(own, landed, part, level, own_at, land_at, land_stride):
        out = sign(part, level, 0) * own[pl.ds(own_at, 8), :]
        for hop in range(3):
            delta = (DELTAS >> (2 * hop)) & 3
            at = land_at + hop * land_stride
            out = out + sign(part, level, delta) * landed[pl.ds(at, 8), :]
        return out

    def fold(own, landed, count, level, copy_in, target, copy_out):
        whole = 4 * count

        for step in range(12):
            part, delta = split_step(step)
            for hop in range(3):
                copy_in(hop * 3 + part, step // 3)

            for t in range(count // 8):
                inside = delta * count + t * 8
                target[pl.ds(step * count + t * 8, 8), :] = total(
                    own, landed, part, level,
                    (9 + part) * whole + inside, part * whole + inside, 3 * whole,
                )
            if step < 9:
                copy_out(step).start()

    def landed1(step, cut):
        copy1(step, cut).wait_recv()

    def landed2(step, cut):
        if cut == 0:
            copy2(step).wait_recv()

    fold(home, land1, 4 * PART, 0, landed1, sum1, copy2)
    fold(sum1, land2, PART, 1, landed2, sum2, copy3)

    for part in range(3):
        for hop in range(3):
            copy3(hop * 3 + part).wait_recv()
        for t in range(PART // 8):
            inside = part * PART + t * 8
            sketch[pl.ds(inside, 8), :] = scale * total(
                sum2, land3, part, 2, 9 * PART + inside, inside, 3 * PART
            )

    rows_here = jnp.concatenate(
        [sketch[:samples, :], jnp.zeros((COLS - samples, COLS), jnp.float32)], axis=0
    )
    turned = jnp.transpose(rows_here)
    device_total = lax.axis_size("hi") * lax.axis_size("lo")
    local = jnp.dot(
        turned, rows_here, precision=lax.Precision.HIGHEST, preferred_element_type=jnp.float32
    ) * (1.0 / (samples * device_total))
    half, quarter = COLS // 2, COLS // 4
    left_half = lax.broadcasted_iota(jnp.int32, (quarter, COLS), 1) < half
    gram[0, :half, :] = local[:half]
    gram[0, half:, :] = jnp.where(
        left_half, pltpu.roll(local[half : half + quarter], half, 1), local[half + quarter :]
    )

    core_gram = send(gram.at[0], core_land, gcs, gcr, other)
    core_gram.start()
    core_gram.wait_recv()
    gram[1] = gram[0] + core_land[...]

    def gram_copy(stage, step):
        part, delta = split_step(step)
        at = stage * 9 + step
        return send(
            block(gram.at[stage + 1], part, GRAM_PART),
            block(gram_land.at[stage * 3 + step // 3], part, GRAM_PART),
            gs.at[at], gr.at[at], peer(part, stage, delta),
        )

    for stage in range(3):
        for step in range(9):
            gram_copy(stage, step).start()
        for part in range(3):
            for hop in range(3):
                gram_copy(stage, hop * 3 + part).wait_recv()
            span = pl.ds(part * GRAM_PART, GRAM_PART)
            own = gram[stage + 1, span, :]
            two, one, three = (gram_land[stage * 3 + hop, span, :] for hop in range(3))
            gram[stage + 2, span, :] = (own + two) + (one + three)

    def put(base, value):
        augmented[base : base + BLOCK, :] = value

    packed = gram[4, half:, :]
    whole_gram = jnp.concatenate(
        [gram[4, :half, :], pltpu.roll(packed, half, 1), packed], axis=0
    )
    eliminate(jnp.concatenate([whole_gram, turned], axis=1), put)
    row_at = lax.broadcasted_iota(jnp.int32, (COLS, COLS), 0)
    col_at = lax.broadcasted_iota(jnp.int32, (COLS, COLS), 1)
    r_ref[...] = jnp.where(row_at <= col_at, augmented[:, :COLS], 0.0)
    q_ref[...] = jnp.transpose(augmented[:, COLS:])[:samples, :]

    for step, cut in order:
        core_copy(step, cut).wait_send()
        if step < 9:
            copy1(step, cut).wait_send()
    for step in range(9):
        for copy in (copy2, copy3):
            copy(step).wait_send()
        for stage in range(3):
            gram_copy(stage, step).wait_send()
    core_gram.wait_send()


def shards(panel, signs, sample_rows):
    rows, cols = panel.shape
    devices = lax.axis_size(("hi", "lo"))
    samples = sample_rows.shape[0] // devices
    f32 = jnp.float32

    def buffers(blocks):
        return pltpu.VMEM((blocks * 3 * PART, cols), f32)

    dma = pltpu.SemaphoreType.DMA
    vmem = pl.BlockSpec(memory_space=pltpu.VMEM)
    hbm = pl.BlockSpec(memory_space=pltpu.HBM)
    return pl.pallas_call(
        functools.partial(kernel, 1.0 / math.sqrt(rows * devices), samples),
        out_shape=(
            pltpu.VMEM((samples, cols), f32),
            pltpu.VMEM((cols, cols), f32),
        ),
        in_specs=[hbm, hbm, hbm],
        out_specs=(vmem, vmem),
        scratch_shapes=[
            pltpu.VMEM((rows, cols), f32),
            pltpu.VMEM((rows, cols), f32),
            pltpu.VMEM((MIX, MIX), jnp.bfloat16),
            pltpu.VMEM((rows // COLS, COLS), jnp.int32),
            pltpu.VMEM(sample_rows.shape, jnp.int32),
            pltpu.SMEM(sample_rows.shape, jnp.int32),
            buffers(64), buffers(64), buffers(64),
            buffers(48), buffers(16), buffers(12), buffers(4), buffers(3),
            pltpu.VMEM((3 * PART, cols), f32),
            pltpu.VMEM((5, 3 * GRAM_PART, cols), f32),
            pltpu.VMEM((9, 3 * GRAM_PART, cols), f32),
            pltpu.VMEM((3 * GRAM_PART, cols), f32),
            pltpu.VMEM((cols, 2 * cols), f32),
            dma((LOADS,)), dma, dma, dma((48,)), dma((48,)),
            dma((36,)), dma((36,)), dma((9,)), dma((9,)), dma((9,)), dma((9,)),
            dma((27,)), dma((27,)), dma, dma,
        ],
        compiler_params=pltpu.CompilerParams(
            collective_id=0, has_side_effects=True, vmem_limit_bytes=63 * 2**20
        ),
        name="sketch_qr",
    )(panel, signs.reshape(rows // COLS, COLS), sample_rows)


def solution(mesh):
    placed = (P(("hi", "lo"), None), P(("hi", "lo")), P())
    return jax.shard_map(
        shards, mesh=mesh, in_specs=placed, out_specs=(P(("hi", "lo"), None), P()), check_vma=False
    )
```

```python
import functools
import math

import jax
import jax.numpy as jnp
from jax import lax
from jax.experimental import pallas as pl
from jax.experimental.pallas import tpu as pltpu
from jax.sharding import PartitionSpec as P

MESH = pl.DeviceIdType.MESH
COLS = 128
MIX = 128
LOADS = 8
BLOCK = 16
PART = 24
GRAM_PART = 32
GATHER_UNROLL = 1
IN_FLIGHT = 4
DELTAS = 0x36
AHEAD = 6


def parity_sign(value, bits):
    total = value & 1
    for place in range(1, bits):
        total = total + ((value >> place) & 1)
    return 1.0 - 2.0 * (total & 1).astype(jnp.float32)


def hadamard(order):
    shape = (order, order)
    common = lax.broadcasted_iota(jnp.int32, shape, 0) & lax.broadcasted_iota(jnp.int32, shape, 1)
    return parity_sign(common, order.bit_length() - 1)


def butterfly(values):
    half = 1
    values = list(values)
    while half < len(values):
        for at in range(len(values)):
            if at & half == 0:
                low, high = values[at], values[at + half]
                values[at], values[at + half] = low + high, low - high
        half *= 2
    return values


def split_three(value):
    first = value.astype(jnp.bfloat16).astype(jnp.float32)
    rest = value - first
    second = rest.astype(jnp.bfloat16).astype(jnp.float32)
    return first, second, rest - second


def widen(value, width):
    return jnp.concatenate([value] * (width // COLS), axis=1)


def eliminate(rest, put):
    order, width = rest.shape
    row_at = lax.broadcasted_iota(jnp.int32, (BLOCK, COLS), 0)
    for step in range(order // BLOCK):
        base = step * BLOCK
        rows = rest[:BLOCK]
        columns = [
            jnp.broadcast_to(rows[:, base + m : base + m + 1], (BLOCK, COLS)) for m in range(BLOCK)
        ]
        pivots = jnp.ones((BLOCK, COLS), jnp.float32)
        for j in range(BLOCK):
            pivot = jnp.broadcast_to(columns[j][j : j + 1, :], (BLOCK, COLS))
            pivots = jnp.where(row_at == j, pivot, pivots)
            if j < BLOCK - 1:
                factor = jnp.where(row_at > j, columns[j] * (1.0 / pivot), 0.0)
                for m in range(j + 1, BLOCK):
                    columns[m] = columns[m] - factor * jnp.broadcast_to(
                        columns[m][j : j + 1, :], (BLOCK, COLS)
                    )
                rows = rows - widen(factor, width) * jnp.broadcast_to(
                    rows[j : j + 1, :], (BLOCK, width)
                )
        done = rows * widen(lax.rsqrt(pivots), width)
        put(base, done)
        if base + BLOCK < order:
            a, b, c = split_three(done)
            left = jnp.concatenate([t[:, :COLS] for t in (a, a, a, b, b, c)], axis=0)
            right = jnp.concatenate([a, b, c, a, b, a], axis=0).astype(jnp.bfloat16)
            turned = jnp.transpose(left)[base + BLOCK :, :].astype(jnp.bfloat16)
            rest = rest[BLOCK:] - jnp.dot(turned, right, preferred_element_type=jnp.float32)


def kernel(
    scale, samples, panel_hbm, sign_hbm, index_hbm, q_ref, r_ref,
    panel, work, mix, sign_ref, index_rows, index, away, near, home, land1, sum1, land2, sum2, land3, sketch,
    gram, gram_land, core_land, augmented,
    load_sem, sign_sem, index_sem, core_send, core_recv, s1, r1, s2, r2, s3, r3, gs, gr, gcs, gcr,
):
    core = lax.axis_index("lo") % 2
    chip = lax.axis_index("hi") * 4 + lax.axis_index("lo") // 2
    rows = panel.shape[0]

    def device(which_chip, which_core):
        return (which_chip // 4, (which_chip % 4) * 2 + which_core)

    def shift(part, level):
        axis = part + level
        return 4 - 2 * (axis % 3) if isinstance(axis, int) else 4 - 2 * lax.rem(axis, 3)

    def peer(part, level, delta):
        return device(chip ^ (delta << shift(part, level)), core)

    def sign(part, level, delta):
        here = (chip >> shift(part, level)) & 3
        return parity_sign(here & (here ^ delta), 2)

    def split_step(step):
        return step % 3, (DELTAS >> (2 * (step // 3))) & 3

    def block(ref, at, count):
        return ref.at[pl.ds(at * count if isinstance(at, int) else pl.multiple_of(at * count, 8), count)]

    other = device(chip, 1 - core)
    barrier = pltpu.get_barrier_semaphore()
    pl.semaphore_signal(barrier, inc=1, device_id=other, device_id_type=MESH)

    def greet(step, carry):
        pl.semaphore_signal(
            barrier, inc=1, device_id=peer(step % 3, 0, step // 3 + 1), device_id_type=MESH
        )
        return carry

    lax.fori_loop(0, 9, greet, 0)

    outer = rows // MIX
    per_load = outer // LOADS
    piece = rows // LOADS

    def load(at):
        span = pl.ds(pl.multiple_of(at * piece, piece), piece)
        return pltpu.make_async_copy(panel_hbm.at[span], panel.at[span], load_sem.at[at])

    sign_copy = pltpu.make_async_copy(sign_hbm, sign_ref, sign_sem)
    sign_copy.start()
    for at in range(IN_FLIGHT):
        load(at).start()
    index_copy = pltpu.make_async_copy(index_hbm, index_rows, index_sem)
    index_copy.start()
    mix[...] = hadamard(MIX).astype(jnp.bfloat16)
    sign_copy.wait()

    def mix_group(at, carry):
        load(at).wait()

        @pl.when(at + IN_FLIGHT < LOADS)
        def _():
            load(at + IN_FLIGHT).start()

        for inner in range(per_load):
            line = at * per_load + inner
            start = pl.multiple_of(line * MIX, MIX)
            value = panel[pl.ds(start, MIX), :]
            high = value.astype(jnp.bfloat16)
            low = (value - high.astype(jnp.float32)).astype(jnp.bfloat16)
            signs = sign_ref[pl.ds(line, 1), :].astype(jnp.float32)
            signed_mix = mix[...] * jnp.broadcast_to(signs, (MIX, MIX)).astype(jnp.bfloat16)
            work[pl.ds(start, MIX), :] = jnp.dot(
                jnp.concatenate([signed_mix, signed_mix], axis=1),
                jnp.concatenate([high, low], axis=0),
                preferred_element_type=jnp.float32,
            )
        return carry

    lax.fori_loop(0, LOADS, mix_group, 0)
    index_copy.wait()
    index_rows[...] = index_rows[...] & (rows - 1)
    index_move = pltpu.make_async_copy(index_rows, index, index_sem)
    index_move.start()

    def butterflies(order, outer_stride, stride, unroll):
        def group(at, carry):
            def tile(t, carry):
                base = pl.multiple_of(at * outer_stride + t * 8, 8)
                spans = [pl.ds(pl.multiple_of(base + m * stride, 8), 8) for m in range(order)]
                for span, value in zip(spans, butterfly([work[span, :] for span in spans])):
                    work[span, :] = value
                return carry

            return lax.fori_loop(0, MIX // 8, tile, carry, unroll=unroll)

        lax.fori_loop(0, outer // order, group, 0)

    butterflies(per_load, per_load * MIX, MIX, 4)
    butterflies(LOADS, MIX, per_load * MIX, 8)
    index_move.wait()

    def gather(step, cut, which, write):
        part, delta = split_step(step)
        count = min(PART, samples - part * PART)

        second = (DELTAS >> (2 * cut)) & 3

        def one(third, carry):
            to_chip = chip ^ (
                (delta << shift(part, 0)) | (second << shift(part, 1)) | (third << shift(part, 2))
            )
            base = (to_chip * 2 + which) * samples + part * PART
            to = pl.multiple_of(step * 16 * PART + (second * 4 + third) * PART, 8)
            for k in range(count):
                write(to + k, work[pl.ds(index[base + k], 1), :])
            return carry

        lax.fori_loop(0, 4, one, 0, unroll=GATHER_UNROLL)

    def send(source, target, send_sem, recv_sem, to):
        return pltpu.make_async_remote_copy(
            src_ref=source, dst_ref=target, send_sem=send_sem, recv_sem=recv_sem,
            device_id=to, device_id_type=MESH,
        )

    def core_copy(step, cut):
        at, size = step * 4 + ((DELTAS >> (2 * cut)) & 3), 4 * PART
        return send(
            block(away, at, size), block(near, at, size),
            core_send.at[at], core_recv.at[at], other,
        )

    def copy1(step, cut):
        part, delta = split_step(step)
        at, size = step * 4 + ((DELTAS >> (2 * cut)) & 3), 4 * PART
        return send(
            block(home, at, size), block(land1, at, size),
            s1.at[at], r1.at[at], peer(part, 0, delta),
        )

    def part_copy(source, target, count, sends, recvs, level, step):
        part, delta = split_step(step)
        return send(
            block(source, step, count), block(target, step, count),
            sends.at[step], recvs.at[step], peer(part, level, delta),
        )

    copy2 = functools.partial(part_copy, sum1, land2, 4 * PART, s2, r2, 1)
    copy3 = functools.partial(part_copy, sum2, land3, PART, s3, r3, 2)
    core_sign = 1.0 - 2.0 * core.astype(jnp.float32)

    def write_away(to, value):
        away[pl.ds(to, 1), :] = value

    def write_home(to, value):
        home[pl.ds(to, 1), :] = near[pl.ds(to, 1), :] + core_sign * value

    pl.semaphore_wait(barrier, 10)

    order = [(hop * 3 + part, cut) for cut in range(4) for hop in range(3) for part in range(3)]
    order += [(9 + part, cut) for part in range(3) for cut in range(4)]
    for at in range(len(order) + AHEAD):
        if at < len(order):
            gather(*order[at], 1 - core, write_away)
            core_copy(*order[at]).start()
        if at >= AHEAD:
            step, cut = order[at - AHEAD]
            core_copy(step, cut).wait_recv()
            gather(step, cut, core, write_home)
            if step < 9:
                copy1(step, cut).start()

    def total(own, landed, part, level, own_at, land_at, land_stride):
        out = sign(part, level, 0) * own[pl.ds(own_at, 8), :]
        for hop in range(3):
            delta = (DELTAS >> (2 * hop)) & 3
            at = land_at + hop * land_stride
            out = out + sign(part, level, delta) * landed[pl.ds(at, 8), :]
        return out

    def fold(own, landed, count, level, copy_in, target, copy_out):
        whole = 4 * count

        for step in range(12):
            part, delta = split_step(step)
            for hop in range(3):
                copy_in(hop * 3 + part, step // 3)

            for t in range(count // 8):
                inside = delta * count + t * 8
                target[pl.ds(step * count + t * 8, 8), :] = total(
                    own, landed, part, level,
                    (9 + part) * whole + inside, part * whole + inside, 3 * whole,
                )
            if step < 9:
                copy_out(step).start()

    def landed1(step, cut):
        copy1(step, cut).wait_recv()

    def landed2(step, cut):
        if cut == 0:
            copy2(step).wait_recv()

    fold(home, land1, 4 * PART, 0, landed1, sum1, copy2)
    fold(sum1, land2, PART, 1, landed2, sum2, copy3)

    for part in range(3):
        for hop in range(3):
            copy3(hop * 3 + part).wait_recv()
        for t in range(PART // 8):
            inside = part * PART + t * 8
            sketch[pl.ds(inside, 8), :] = scale * total(
                sum2, land3, part, 2, 9 * PART + inside, inside, 3 * PART
            )

    rows_here = jnp.concatenate(
        [sketch[:samples, :], jnp.zeros((COLS - samples, COLS), jnp.float32)], axis=0
    )
    turned = jnp.transpose(rows_here)
    device_total = lax.axis_size("hi") * lax.axis_size("lo")
    local = jnp.dot(
        turned, rows_here, precision=lax.Precision.HIGHEST, preferred_element_type=jnp.float32
    ) * (1.0 / (samples * device_total))
    half, quarter = COLS // 2, COLS // 4
    left_half = lax.broadcasted_iota(jnp.int32, (quarter, COLS), 1) < half
    gram[0, :half, :] = local[:half]
    gram[0, half:, :] = jnp.where(
        left_half, pltpu.roll(local[half : half + quarter], half, 1), local[half + quarter :]
    )

    core_gram = send(gram.at[0], core_land, gcs, gcr, other)
    core_gram.start()
    core_gram.wait_recv()
    gram[1] = gram[0] + core_land[...]

    def gram_copy(stage, step):
        part, delta = split_step(step)
        at = stage * 9 + step
        return send(
            block(gram.at[stage + 1], part, GRAM_PART),
            block(gram_land.at[stage * 3 + step // 3], part, GRAM_PART),
            gs.at[at], gr.at[at], peer(part, stage, delta),
        )

    for step in range(9):
        gram_copy(0, step).start()
    for step, cut in order:
        core_copy(step, cut).wait_send()
        if step < 9:
            copy1(step, cut).wait_send()
    for step in range(9):
        for copy in (copy2, copy3):
            copy(step).wait_send()
    core_gram.wait_send()
    for stage in range(3):
        for part in range(3):
            for hop in range(3):
                gram_copy(stage, hop * 3 + part).wait_recv()
            span = pl.ds(part * GRAM_PART, GRAM_PART)
            own = gram[stage + 1, span, :]
            two, one, three = (gram_land[stage * 3 + hop, span, :] for hop in range(3))
            gram[stage + 2, span, :] = (own + two) + (one + three)
            if stage < 2:
                for hop in range(3):
                    gram_copy(stage + 1, hop * 3 + part).start()
        for step in range(9):
            gram_copy(stage, step).wait_send()

    def put(base, value):
        augmented[base : base + BLOCK, :] = value

    packed = gram[4, half:, :]
    whole_gram = jnp.concatenate(
        [gram[4, :half, :], pltpu.roll(packed, half, 1), packed], axis=0
    )
    eliminate(jnp.concatenate([whole_gram, turned], axis=1), put)
    row_at = lax.broadcasted_iota(jnp.int32, (COLS, COLS), 0)
    col_at = lax.broadcasted_iota(jnp.int32, (COLS, COLS), 1)
    r_ref[...] = jnp.where(row_at <= col_at, augmented[:, :COLS], 0.0)
    q_ref[...] = jnp.transpose(augmented[:, COLS:])[:samples, :]


def shards(panel, signs, sample_rows):
    rows, cols = panel.shape
    devices = lax.axis_size(("hi", "lo"))
    samples = sample_rows.shape[0] // devices
    f32 = jnp.float32

    def buffers(blocks):
        return pltpu.VMEM((blocks * 3 * PART, cols), f32)

    dma = pltpu.SemaphoreType.DMA
    vmem = pl.BlockSpec(memory_space=pltpu.VMEM)
    hbm = pl.BlockSpec(memory_space=pltpu.HBM)
    return pl.pallas_call(
        functools.partial(kernel, 1.0 / math.sqrt(rows * devices), samples),
        out_shape=(
            pltpu.VMEM((samples, cols), f32),
            pltpu.VMEM((cols, cols), f32),
        ),
        in_specs=[hbm, hbm, hbm],
        out_specs=(vmem, vmem),
        scratch_shapes=[
            pltpu.VMEM((rows, cols), f32),
            pltpu.VMEM((rows, cols), f32),
            pltpu.VMEM((MIX, MIX), jnp.bfloat16),
            pltpu.VMEM((rows // COLS, COLS), jnp.int32),
            pltpu.VMEM(sample_rows.shape, jnp.int32),
            pltpu.SMEM(sample_rows.shape, jnp.int32),
            buffers(64), buffers(64), buffers(64),
            buffers(48), buffers(16), buffers(12), buffers(4), buffers(3),
            pltpu.VMEM((3 * PART, cols), f32),
            pltpu.VMEM((5, 3 * GRAM_PART, cols), f32),
            pltpu.VMEM((9, 3 * GRAM_PART, cols), f32),
            pltpu.VMEM((3 * GRAM_PART, cols), f32),
            pltpu.VMEM((cols, 2 * cols), f32),
            dma((LOADS,)), dma, dma, dma((48,)), dma((48,)),
            dma((36,)), dma((36,)), dma((9,)), dma((9,)), dma((9,)), dma((9,)),
            dma((27,)), dma((27,)), dma, dma,
        ],
        compiler_params=pltpu.CompilerParams(
            collective_id=0, has_side_effects=True, vmem_limit_bytes=63 * 2**20
        ),
        name="sketch_qr",
    )(panel, signs.reshape(rows // COLS, COLS), sample_rows)


def solution(mesh):
    placed = (P(("hi", "lo"), None), P(("hi", "lo")), P())
    return jax.shard_map(
        shards, mesh=mesh, in_specs=placed, out_specs=(P(("hi", "lo"), None), P()), check_vma=False
    )
```

```python
import functools
import math

import jax
import jax.numpy as jnp
from jax import lax
from jax.experimental import pallas as pl
from jax.experimental.pallas import tpu as pltpu
from jax.sharding import PartitionSpec as P

MESH = pl.DeviceIdType.MESH
COLS = 128
MIX = 128
LOADS = 8
BLOCK = 16
PART = 24
GRAM_PART = 32
GATHER_UNROLL = 1
IN_FLIGHT = 4
DELTAS = 0x36
AHEAD = 6


def parity_sign(value, bits):
    total = value & 1
    for place in range(1, bits):
        total = total + ((value >> place) & 1)
    return 1.0 - 2.0 * (total & 1).astype(jnp.float32)


def hadamard(order):
    shape = (order, order)
    common = lax.broadcasted_iota(jnp.int32, shape, 0) & lax.broadcasted_iota(jnp.int32, shape, 1)
    return parity_sign(common, order.bit_length() - 1)


def butterfly(values):
    half = 1
    values = list(values)
    while half < len(values):
        for at in range(len(values)):
            if at & half == 0:
                low, high = values[at], values[at + half]
                values[at], values[at + half] = low + high, low - high
        half *= 2
    return values


def split_three(value):
    first = value.astype(jnp.bfloat16).astype(jnp.float32)
    rest = value - first
    second = rest.astype(jnp.bfloat16).astype(jnp.float32)
    return first, second, rest - second


def widen(value, width):
    return jnp.concatenate([value] * (width // COLS), axis=1)


def eliminate(rest, put):
    order, width = rest.shape
    row_at = lax.broadcasted_iota(jnp.int32, (BLOCK, COLS), 0)
    for step in range(order // BLOCK):
        base = step * BLOCK
        rows = rest[:BLOCK]
        columns = [
            jnp.broadcast_to(rows[:, base + m : base + m + 1], (BLOCK, COLS)) for m in range(BLOCK)
        ]
        pivots = jnp.ones((BLOCK, COLS), jnp.float32)
        for j in range(BLOCK):
            pivot = jnp.broadcast_to(columns[j][j : j + 1, :], (BLOCK, COLS))
            pivots = jnp.where(row_at == j, pivot, pivots)
            if j < BLOCK - 1:
                factor = jnp.where(row_at > j, columns[j] * (1.0 / pivot), 0.0)
                for m in range(j + 1, BLOCK):
                    columns[m] = columns[m] - factor * jnp.broadcast_to(
                        columns[m][j : j + 1, :], (BLOCK, COLS)
                    )
                rows = rows - widen(factor, width) * jnp.broadcast_to(
                    rows[j : j + 1, :], (BLOCK, width)
                )
        done = rows * widen(lax.rsqrt(pivots), width)
        put(base, done)
        if base + BLOCK < order:
            a, b, c = split_three(done)
            left = jnp.concatenate([t[:, :COLS] for t in (a, a, a, b, b, c)], axis=0)
            right = jnp.concatenate([a, b, c, a, b, a], axis=0).astype(jnp.bfloat16)
            turned = jnp.transpose(left)[base + BLOCK :, :].astype(jnp.bfloat16)
            rest = rest[BLOCK:] - jnp.dot(turned, right, preferred_element_type=jnp.float32)


def kernel(
    scale, samples, panel_hbm, sign_hbm, index_hbm, q_ref, r_ref,
    panel, work, mix, sign_ref, index_rows, index, away, near, home, land1, sum1, land2, sum2, land3, sketch,
    gram, gram_land, core_land, augmented,
    load_sem, sign_sem, index_sem, core_send, core_recv, s1, r1, s2, r2, s3, r3, gs, gr, gcs, gcr,
):
    core = lax.axis_index("lo") % 2
    chip = lax.axis_index("hi") * 4 + lax.axis_index("lo") // 2
    rows = panel.shape[0]

    def device(which_chip, which_core):
        return (which_chip // 4, (which_chip % 4) * 2 + which_core)

    def shift(part, level):
        axis = part + level
        return 4 - 2 * (axis % 3) if isinstance(axis, int) else 4 - 2 * lax.rem(axis, 3)

    def peer(part, level, delta):
        return device(chip ^ (delta << shift(part, level)), core)

    def sign(part, level, delta):
        here = (chip >> shift(part, level)) & 3
        return parity_sign(here & (here ^ delta), 2)

    def split_step(step):
        return step % 3, (DELTAS >> (2 * (step // 3))) & 3

    def block(ref, at, count):
        return ref.at[pl.ds(at * count if isinstance(at, int) else pl.multiple_of(at * count, 8), count)]

    outer = rows // MIX
    per_load = outer // LOADS
    piece = rows // LOADS

    def load(at):
        span = pl.ds(pl.multiple_of(at * piece, piece), piece)
        return pltpu.make_async_copy(panel_hbm.at[span], panel.at[span], load_sem.at[at])

    sign_copy = pltpu.make_async_copy(sign_hbm, sign_ref, sign_sem)
    sign_copy.start()
    for at in range(IN_FLIGHT):
        load(at).start()
    index_copy = pltpu.make_async_copy(index_hbm, index_rows, index_sem)
    index_copy.start()
    other = device(chip, 1 - core)
    barrier = pltpu.get_barrier_semaphore()
    pl.semaphore_signal(barrier, inc=1, device_id=other, device_id_type=MESH)

    for part in range(3):
        for delta in range(1, 4):
            pl.semaphore_signal(
                barrier, inc=1, device_id=peer(part, 0, delta), device_id_type=MESH
            )

    mix[...] = hadamard(MIX).astype(jnp.bfloat16)
    sign_copy.wait()

    def mix_group(at, carry):
        load(at).wait()

        @pl.when(at + IN_FLIGHT < LOADS)
        def _():
            load(at + IN_FLIGHT).start()

        for inner in range(per_load):
            line = at * per_load + inner
            start = pl.multiple_of(line * MIX, MIX)
            value = panel[pl.ds(start, MIX), :]
            high = value.astype(jnp.bfloat16)
            low = (value - high.astype(jnp.float32)).astype(jnp.bfloat16)
            signs = sign_ref[pl.ds(line, 1), :].astype(jnp.float32)
            signed_mix = mix[...] * jnp.broadcast_to(signs, (MIX, MIX)).astype(jnp.bfloat16)
            work[pl.ds(start, MIX), :] = jnp.dot(
                jnp.concatenate([signed_mix, signed_mix], axis=1),
                jnp.concatenate([high, low], axis=0),
                preferred_element_type=jnp.float32,
            )
        return carry

    lax.fori_loop(0, LOADS, mix_group, 0)
    index_copy.wait()
    index_rows[...] = index_rows[...] & (rows - 1)
    index_move = pltpu.make_async_copy(index_rows, index, index_sem)
    index_move.start()

    def butterflies(order, outer_stride, stride, unroll):
        def group(at, carry):
            def tile(t, carry):
                base = pl.multiple_of(at * outer_stride + t * 8, 8)
                spans = [pl.ds(pl.multiple_of(base + m * stride, 8), 8) for m in range(order)]
                for span, value in zip(spans, butterfly([work[span, :] for span in spans])):
                    work[span, :] = value
                return carry

            return lax.fori_loop(0, MIX // 8, tile, carry, unroll=unroll)

        lax.fori_loop(0, outer // order, group, 0)

    butterflies(per_load, per_load * MIX, MIX, 4)
    butterflies(LOADS, MIX, per_load * MIX, 8)
    index_move.wait()

    def gather(step, cut, which, write):
        part, delta = split_step(step)
        count = min(PART, samples - part * PART)

        second = (DELTAS >> (2 * cut)) & 3

        def one(third, carry):
            to_chip = chip ^ (
                (delta << shift(part, 0)) | (second << shift(part, 1)) | (third << shift(part, 2))
            )
            base = (to_chip * 2 + which) * samples + part * PART
            to = pl.multiple_of(step * 16 * PART + (second * 4 + third) * PART, 8)
            for k in range(count):
                write(to + k, work[pl.ds(index[base + k], 1), :])
            return carry

        lax.fori_loop(0, 4, one, 0, unroll=GATHER_UNROLL)

    def send(source, target, send_sem, recv_sem, to):
        return pltpu.make_async_remote_copy(
            src_ref=source, dst_ref=target, send_sem=send_sem, recv_sem=recv_sem,
            device_id=to, device_id_type=MESH,
        )

    def core_copy(step, cut):
        at, size = step * 4 + ((DELTAS >> (2 * cut)) & 3), 4 * PART
        return send(
            block(away, at, size), block(near, at, size),
            core_send.at[at], core_recv.at[at], other,
        )

    def copy1(step, cut):
        part, delta = split_step(step)
        at, size = step * 4 + ((DELTAS >> (2 * cut)) & 3), 4 * PART
        return send(
            block(home, at, size), block(land1, at, size),
            s1.at[at], r1.at[at], peer(part, 0, delta),
        )

    def part_copy(source, target, count, sends, recvs, level, step):
        part, delta = split_step(step)
        return send(
            block(source, step, count), block(target, step, count),
            sends.at[step], recvs.at[step], peer(part, level, delta),
        )

    copy2 = functools.partial(part_copy, sum1, land2, 4 * PART, s2, r2, 1)
    copy3 = functools.partial(part_copy, sum2, land3, PART, s3, r3, 2)
    core_sign = 1.0 - 2.0 * core.astype(jnp.float32)

    def write_away(to, value):
        away[pl.ds(to, 1), :] = value

    def write_home(to, value):
        home[pl.ds(to, 1), :] = near[pl.ds(to, 1), :] + core_sign * value

    pl.semaphore_wait(barrier, 10)

    order = [(hop * 3 + part, cut) for cut in range(4) for hop in range(3) for part in range(3)]
    order += [(9 + part, cut) for part in range(3) for cut in range(4)]
    for at in range(len(order) + AHEAD):
        if at < len(order):
            gather(*order[at], 1 - core, write_away)
            core_copy(*order[at]).start()
        if at >= AHEAD:
            step, cut = order[at - AHEAD]
            core_copy(step, cut).wait_recv()
            gather(step, cut, core, write_home)
            if step < 9:
                copy1(step, cut).start()

    def total(own, landed, part, level, own_at, land_at, land_stride):
        out = sign(part, level, 0) * own[pl.ds(own_at, 8), :]
        for hop in range(3):
            delta = (DELTAS >> (2 * hop)) & 3
            at = land_at + hop * land_stride
            out = out + sign(part, level, delta) * landed[pl.ds(at, 8), :]
        return out

    def fold(own, landed, count, level, copy_in, target, copy_out):
        whole = 4 * count

        for step in range(12):
            part, delta = split_step(step)
            for hop in range(3):
                copy_in(hop * 3 + part, step // 3)

            for t in range(count // 8):
                inside = delta * count + t * 8
                target[pl.ds(step * count + t * 8, 8), :] = total(
                    own, landed, part, level,
                    (9 + part) * whole + inside, part * whole + inside, 3 * whole,
                )
            if step < 9:
                copy_out(step).start()

    def landed1(step, cut):
        copy1(step, cut).wait_recv()

    def landed2(step, cut):
        if cut == 0:
            copy2(step).wait_recv()

    fold(home, land1, 4 * PART, 0, landed1, sum1, copy2)
    fold(sum1, land2, PART, 1, landed2, sum2, copy3)

    for part in range(3):
        for hop in range(3):
            copy3(hop * 3 + part).wait_recv()
        for t in range(PART // 8):
            inside = part * PART + t * 8
            sketch[pl.ds(inside, 8), :] = scale * total(
                sum2, land3, part, 2, 9 * PART + inside, inside, 3 * PART
            )

    rows_here = jnp.concatenate(
        [sketch[:samples, :], jnp.zeros((COLS - samples, COLS), jnp.float32)], axis=0
    )
    turned = jnp.transpose(rows_here)
    device_total = lax.axis_size("hi") * lax.axis_size("lo")
    local = jnp.dot(
        turned, rows_here, precision=lax.Precision.HIGHEST, preferred_element_type=jnp.float32
    ) * (1.0 / (samples * device_total))
    half, quarter = COLS // 2, COLS // 4
    left_half = lax.broadcasted_iota(jnp.int32, (quarter, COLS), 1) < half
    gram[0, :half, :] = local[:half]
    gram[0, half:, :] = jnp.where(
        left_half, pltpu.roll(local[half : half + quarter], half, 1), local[half + quarter :]
    )

    core_gram = send(gram.at[0], core_land, gcs, gcr, other)
    core_gram.start()
    core_gram.wait_recv()
    gram[1] = gram[0] + core_land[...]

    def gram_copy(stage, step):
        part, delta = split_step(step)
        at = stage * 9 + step
        return send(
            block(gram.at[stage + 1], part, GRAM_PART),
            block(gram_land.at[stage * 3 + step // 3], part, GRAM_PART),
            gs.at[at], gr.at[at], peer(part, stage, delta),
        )

    for step in range(9):
        gram_copy(0, step).start()
    for step, cut in order:
        core_copy(step, cut).wait_send()
        if step < 9:
            copy1(step, cut).wait_send()
    for step in range(9):
        for copy in (copy2, copy3):
            copy(step).wait_send()
    core_gram.wait_send()
    for stage in range(3):
        for part in range(3):
            for hop in range(3):
                gram_copy(stage, hop * 3 + part).wait_recv()
            span = pl.ds(part * GRAM_PART, GRAM_PART)
            own = gram[stage + 1, span, :]
            two, one, three = (gram_land[stage * 3 + hop, span, :] for hop in range(3))
            gram[stage + 2, span, :] = (own + two) + (one + three)
            if stage < 2:
                for hop in range(3):
                    gram_copy(stage + 1, hop * 3 + part).start()
        for step in range(9):
            gram_copy(stage, step).wait_send()

    def put(base, value):
        augmented[base : base + BLOCK, :] = value

    packed = gram[4, half:, :]
    whole_gram = jnp.concatenate(
        [gram[4, :half, :], pltpu.roll(packed, half, 1), packed], axis=0
    )
    eliminate(jnp.concatenate([whole_gram, turned], axis=1), put)
    row_at = lax.broadcasted_iota(jnp.int32, (COLS, COLS), 0)
    col_at = lax.broadcasted_iota(jnp.int32, (COLS, COLS), 1)
    r_ref[...] = jnp.where(row_at <= col_at, augmented[:, :COLS], 0.0)
    q_ref[...] = jnp.transpose(augmented[:, COLS:])[:samples, :]


def shards(panel, signs, sample_rows):
    rows, cols = panel.shape
    devices = lax.axis_size(("hi", "lo"))
    samples = sample_rows.shape[0] // devices
    f32 = jnp.float32

    def buffers(blocks):
        return pltpu.VMEM((blocks * 3 * PART, cols), f32)

    dma = pltpu.SemaphoreType.DMA
    vmem = pl.BlockSpec(memory_space=pltpu.VMEM)
    hbm = pl.BlockSpec(memory_space=pltpu.HBM)
    return pl.pallas_call(
        functools.partial(kernel, 1.0 / math.sqrt(rows * devices), samples),
        out_shape=(
            pltpu.VMEM((samples, cols), f32),
            pltpu.VMEM((cols, cols), f32),
        ),
        in_specs=[hbm, hbm, hbm],
        out_specs=(vmem, vmem),
        scratch_shapes=[
            pltpu.VMEM((rows, cols), f32),
            pltpu.VMEM((rows, cols), f32),
            pltpu.VMEM((MIX, MIX), jnp.bfloat16),
            pltpu.VMEM((rows // COLS, COLS), jnp.int32),
            pltpu.VMEM(sample_rows.shape, jnp.int32),
            pltpu.SMEM(sample_rows.shape, jnp.int32),
            buffers(64), buffers(64), buffers(64),
            buffers(48), buffers(16), buffers(12), buffers(4), buffers(3),
            pltpu.VMEM((3 * PART, cols), f32),
            pltpu.VMEM((5, 3 * GRAM_PART, cols), f32),
            pltpu.VMEM((9, 3 * GRAM_PART, cols), f32),
            pltpu.VMEM((3 * GRAM_PART, cols), f32),
            pltpu.VMEM((cols, 2 * cols), f32),
            dma((LOADS,)), dma, dma, dma((48,)), dma((48,)),
            dma((36,)), dma((36,)), dma((9,)), dma((9,)), dma((9,)), dma((9,)),
            dma((27,)), dma((27,)), dma, dma,
        ],
        compiler_params=pltpu.CompilerParams(
            collective_id=0, has_side_effects=True, vmem_limit_bytes=63 * 2**20
        ),
        name="sketch_qr",
    )(panel, signs.reshape(rows // COLS, COLS), sample_rows)


def solution(mesh):
    placed = (P(("hi", "lo"), None), P(("hi", "lo")), P())
    return jax.shard_map(
        shards, mesh=mesh, in_specs=placed, out_specs=(P(("hi", "lo"), None), P()), check_vma=False
    )
```
